32 devices in a mesh: groups: 2 (over x), epoch: 16 (over z, y, core).
Axes of the slice: x: 2, y: 2, z: 4, core: 2. Of those that a mesh axis runs over, the one named last changes fastest.
Arguments:
- science: bfloat16 [32, 256, 384], P(('groups', 'epoch')), parts along dimension 0, may hold values from -6 to 6
- template: bfloat16 [512, 384], P(('groups', 'epoch')), parts along dimension 0, may hold values from -6 to 6
- kernels: bfloat16 [16, 21, 21], replicated, may hold values from -0.25 to 0.25
- coef: float32 [32, 8, 16], P(('groups', 'epoch')), parts along dimension 0, may hold values from -1.5 to 1.5
- grid_index: int32 [32, 2, 3], P(('groups', 'epoch')), parts along dimension 0, may hold values from 0 to 7
- clip_mask: int32 [32, 256, 384], P('groups', 'epoch'), parts along dimension 0, may hold values 0 or 1
- inv_var: bfloat16 [32, 256, 384], P('groups', 'epoch'), parts along dimension 0, may hold values from 0.25 to 4
Outputs:
- significance: float32 [512, 384], P(('groups', 'epoch')), parts along dimension 0
The draws below stay inside these ranges and needn't reach their ends.
There are 2 independent parts, one for each index of `groups`. The reference program is written for one: setup_inputs(seed, part) draws one part's arguments, and reference() takes and returns one part's arrays. A program takes and returns all parts, laid end to end along the dimension named above; an argument that names none is the same for every part. Nothing has to cross between parts.
All inputs are finite; a program needn't handle non-finite values. No bound on the sum of `clip_mask` on one device may be relied on, other than what follows from the above.
Results may differ from the reference program's by a relative error of at most 0.0039.
Values may be sent and summed in bfloat16 or wider, within the bound.
No kernel may reach another device: no remote copies, remote signals or barrier semaphores. Data moves between devices by JAX's collectives and lax.ppermute only.
A program may use at most 128 MiB of HBM per device.

```python
import math
import jax
import jax.numpy as jnp
from jax import lax

W = 384
H_DEV = 16
NB = 16
KSIZE = 21
NGRID = 8
CELL = 128
ITERS = 3
HALF = 10
EPOCHS = 16
H = 256
GR = 2
GC = 3


def set_ends(values, key, low, top_value):
    spot = [jax.random.randint(jax.random.fold_in(key, axis), (), 0, length) for axis, length in enumerate(values.shape)]
    widest = values.shape.index(max(values.shape))
    neighbour = spot[:widest] + [(spot[widest] + 1) % values.shape[widest]] + spot[widest + 1:]
    return values.at[tuple(spot)].set(low).at[tuple(neighbour)].set(top_value)


def shard_levels(own_key, extent, pieces, low, high):
    def one(dim, blocks):
        steps = jax.random.uniform(jax.random.fold_in(jax.random.fold_in(own_key, 6), dim), (blocks,), jnp.float32, low / len(pieces), high / len(pieces))
        return jnp.repeat(jnp.exp(steps), extent[dim] // blocks).reshape((-1,) + (1,) * (len(extent) - dim - 1))

    loudness = one(*pieces[0])
    for cut in pieces[1:]:
        loudness = loudness * one(*cut)
    return loudness


def scatter_about(stream_key, dims, deviation, most, split=(), kind=jnp.bfloat16):
    result = jax.random.normal(stream_key, dims, jnp.float32) * deviation
    if len(split) > 0:
        result = shard_levels(stream_key, dims, split, -0.22, 0.18) * result
    return jnp.clip(result, min=-most, max=most).astype(kind)


def setup_inputs(seed: int = 0, part: int = 0) -> dict:
    seeds = jax.random.split(jax.random.key(seed), 8)
    own_keys = jax.random.split(jax.random.fold_in(seeds[7], part), 8)
    return {
        "science": scatter_about(own_keys[0], (EPOCHS, H, W), 1.0, 6.0, ((0, 16),)),
        "template": scatter_about(own_keys[1], (H, W), 1.0, 6.0, ((0, 16),)),
        "kernels": scatter_about(seeds[2], (NB, KSIZE, KSIZE), (KSIZE * KSIZE) ** -0.5, 0.25),
        "coef": scatter_about(own_keys[3], (EPOCHS, NGRID, NB), 0.25, 1.5, ((0, 16),), jnp.float32),
        "grid_index": set_ends(jax.random.randint(own_keys[4], (EPOCHS, GR, GC), 0, NGRID), jax.random.fold_in(own_keys[4], 1), 0, NGRID - 1).astype(jnp.int32),
        "clip_mask": set_ends((jax.random.randint(own_keys[5], (EPOCHS, H, W), 0, 8) < 7).astype(jnp.int32), jax.random.fold_in(own_keys[5], 1), 0, 1),
        "inv_var": jnp.clip(jnp.exp(math.log(4.0) - 2.7725887 * jax.random.uniform(own_keys[6], (EPOCHS, H, W), jnp.float32) ** shard_levels(own_keys[6], (EPOCHS, H, W), ((1, 16),), -0.2, 0.2)), 0.25, 4.0).astype(jnp.bfloat16),
    }


def basis_block(padded_rows, kernels):
    out = lax.conv_general_dilated(padded_rows[None, None], kernels[:, None], (1, 1), 'VALID', preferred_element_type=jnp.float32)
    return out[0].astype(jnp.bfloat16)

def cell_table(coef, grid_index):
    levels = jnp.arange(coef.shape[1], dtype=jnp.int32)
    onehot = (grid_index[..., None] == levels).astype(jnp.float32)
    return jnp.einsum('egcn,enk->ekgc', onehot, coef.astype(jnp.float32), precision=lax.Precision.HIGHEST)

def difference_rows(science, table, basis, start):
    rows = basis.shape[1]
    width = basis.shape[2]
    row_cell = (start + jnp.arange(rows, dtype=jnp.int32)) // CELL
    pick_rows = (row_cell[:, None] == jnp.arange(table.shape[2], dtype=jnp.int32)[None, :]).astype(jnp.float32)
    col_cell = jnp.arange(width, dtype=jnp.int32) // CELL
    pick_cols = (col_cell[:, None] == jnp.arange(table.shape[3], dtype=jnp.int32)[None, :]).astype(jnp.float32)
    coef_map = jnp.einsum('ekgc,rg,wc->ekrw', table, pick_rows, pick_cols, precision=lax.Precision.HIGHEST)
    model = lax.optimization_barrier(jnp.sum(coef_map * basis.astype(jnp.float32)[None], axis=1))
    local_sci = lax.dynamic_slice_in_dim(science, start, rows, 1).astype(jnp.float32)
    return (local_sci - model).astype(jnp.bfloat16)

def stack_pixels(difference, clip_mask, inv_var):
    values = difference.astype(jnp.float32)
    weight_iv = inv_var.astype(jnp.float32)
    base = clip_mask.astype(jnp.float32) * weight_iv
    num = lax.optimization_barrier(jnp.sum(base * values, axis=0))
    den = lax.optimization_barrier(jnp.sum(base, axis=0))
    mean = num / (1.0 + den)
    for sweep in range(ITERS):
        resid = values - mean[None]
        weight = base / (1.0 + weight_iv * resid * resid)
        num = lax.optimization_barrier(jnp.sum(weight * values, axis=0))
        den = lax.optimization_barrier(jnp.sum(weight, axis=0))
        mean = num / (1.0 + den)
    return num / jnp.sqrt(1.0 + den)

def reference(science, template, kernels, coef, grid_index, clip_mask, inv_var):
    padded = jnp.pad(template, ((HALF, HALF), (HALF, HALF)))
    basis = basis_block(padded, kernels)
    table = cell_table(coef, grid_index)

    def one_epoch(pair):
        return difference_rows(pair[0][None], pair[1][None], basis, 0)[0]
    difference = lax.map(one_epoch, (science, table))
    epochs = difference.shape[0]
    height = difference.shape[1]
    width = difference.shape[2]
    parts = height // H_DEV

    def regroup(array):
        return jnp.moveaxis(array.reshape(epochs, parts, H_DEV, width), 1, 0)
    stacked = lax.map(lambda trio: stack_pixels(trio[0], trio[1], trio[2]), (regroup(difference), regroup(clip_mask), regroup(inv_var)))
    return stacked.reshape(height, width)
```

```python
import functools

import jax
import jax.numpy as jnp
from jax import lax
from jax.experimental import pallas as pl
from jax.experimental.pallas import tpu as pltpu
from jax.sharding import PartitionSpec as P

CELL = 128
ITERS = 3
LANES = 128
SUB = 8
TILE = 16
VMEM_LIMIT = 16 * 1024 * 1024


def up(value, unit):
    return -(-value // unit) * unit


def tree_sum(items):
    items = list(items)
    while len(items) > 1:
        items = [
            items[i] + items[i + 1] if i + 1 < len(items) else items[i]
            for i in range(0, len(items), 2)
        ]
    return items[0]


def pack_kernel(rows, science, coef, grid_index, out, spread):
    height, width = science.shape[1:]
    columns = width // CELL
    basis = coef.shape[2]
    spread[...] = jnp.zeros(spread.shape, jnp.float32)
    spread[:, :basis] = coef[0]
    tail = out.shape[1] - columns * rows
    for cell_row in range(grid_index.shape[1]):
        picked = [
            spread[pl.ds(grid_index[0, cell_row, c], 1), :] for c in range(columns)
        ]
        block = jnp.concatenate(
            picked + [jnp.zeros((tail - columns, LANES), jnp.float32)], axis=0
        )
        first = block.astype(jnp.bfloat16).astype(jnp.float32)
        rest = block - first
        second = rest.astype(jnp.bfloat16).astype(jnp.float32)
        third = rest - second
        block = first + pltpu.roll(second, basis, 1) + pltpu.roll(third, 2 * basis, 1)
        block = block.astype(jnp.bfloat16)
        for d in range(cell_row * CELL // rows, (cell_row + 1) * CELL // rows):
            out[d, columns * rows :, :] = block
    for d in range(height // rows):
        for c in range(columns):
            out[d, c * rows : (c + 1) * rows, :] = science[
                0, d * rows : (d + 1) * rows, c * CELL : (c + 1) * CELL
            ]


def pack(science, coef, grid_index, rows):
    height, width = science.shape[1:]
    columns = width // CELL
    return pl.pallas_call(
        functools.partial(pack_kernel, rows),
        out_shape=jax.ShapeDtypeStruct(
            (height // rows, columns * rows + TILE, LANES), jnp.bfloat16
        ),
        in_specs=[
            pl.BlockSpec(memory_space=pltpu.VMEM),
            pl.BlockSpec(memory_space=pltpu.VMEM),
            pl.BlockSpec(memory_space=pltpu.SMEM),
        ],
        scratch_shapes=[pltpu.VMEM((up(coef.shape[1], SUB), LANES), jnp.float32)],
        compiler_params=pltpu.CompilerParams(vmem_limit_bytes=VMEM_LIMIT),
        cost_estimate=pl.CostEstimate(flops=0, bytes_accessed=500_000, transcendentals=0),
    )(science, coef, grid_index)


def basis_kernel(slot, kernels, own, pair, other, out, image, taps, turned, left, right):
    count, side, _ = kernels.shape
    half = side // 2
    rows, width = own.shape
    span = image.shape[1]
    odd = lax.rem(lax.axis_index("epoch"), 2) == 1
    image[...] = jnp.zeros(image.shape, jnp.float32)
    below = pair[...].astype(jnp.float32)
    above = other[...].astype(jnp.float32)
    low = jnp.where(odd, below, above)
    high = jnp.where(odd, above, below)
    image[:half, :width] = low[rows - half :, :]
    image[half : half + rows, :width] = own[...].astype(jnp.float32)
    image[half + rows : 2 * half + rows, :width] = high[:half, :]
    image[...] = pltpu.roll(image[...], (span + half + 1 - slot) % span, 1)
    taps[...] = jnp.zeros(taps.shape, jnp.float32)
    taps[:, :side, :side] = kernels[...].astype(jnp.float32)
    flip = (
        lax.broadcasted_iota(jnp.int32, (LANES, LANES), 0)
        + lax.broadcasted_iota(jnp.int32, (LANES, LANES), 1)
        == slot - 1
    )
    flat = taps[...].reshape(count * taps.shape[1], LANES).astype(jnp.bfloat16)
    turned[...] = jnp.dot(
        flat, flip.astype(jnp.bfloat16), preferred_element_type=jnp.float32
    ).reshape(turned.shape)
    per = LANES // slot
    lines = [turned[:, u, :] for u in range(side)]
    left[...] = jnp.zeros(left.shape, jnp.bfloat16)
    for phase in range(min(per, rows)):
        chunks = {}
        for u in range(side):
            chunk, place = divmod(u + phase, per)
            line = lines[u] if place == 0 else pltpu.roll(lines[u], place * slot, 1)
            chunks[chunk] = line if chunk not in chunks else chunks[chunk] + line
        for y in range(phase, rows, per):
            for chunk, value in chunks.items():
                at = (y // per + chunk) * LANES
                left[y * count : (y + 1) * count, at : at + LANES] = value.astype(jnp.bfloat16)
    for row in range(rows + 2 * half):
        line = jnp.broadcast_to(image[row : row + 1, :], (slot, span))
        moved = pltpu.roll(line, 0, 1, stride=1, stride_axis=0)
        right[row * slot : (row + 1) * slot, :] = moved[:, :width].astype(jnp.bfloat16)
    out[...] = jnp.dot(
        left[...], right[...], preferred_element_type=jnp.float32
    ).astype(jnp.bfloat16)


def basis_rows(kernels, own, pair, other):
    count, side, _ = kernels.shape
    rows, width = own.shape
    slot = up(side, 32)
    lines = rows + side - 1
    span = up(width + side, LANES)
    depth = up(lines * slot, LANES)
    return pl.pallas_call(
        functools.partial(basis_kernel, slot),
        out_shape=jax.ShapeDtypeStruct((rows * count, width), jnp.bfloat16),
        scratch_shapes=[
            pltpu.VMEM((up(lines, SUB), span), jnp.float32),
            pltpu.VMEM((count, up(side, SUB), LANES), jnp.float32),
            pltpu.VMEM((count, up(side, SUB), LANES), jnp.float32),
            pltpu.VMEM((rows * count, depth), jnp.bfloat16),
            pltpu.VMEM((depth, width), jnp.bfloat16),
        ],
        compiler_params=pltpu.CompilerParams(vmem_limit_bytes=VMEM_LIMIT),
        cost_estimate=pl.CostEstimate(
            flops=2 * rows * count * depth * width, bytes_accessed=600_000, transcendentals=0
        ),
    )(kernels, own, pair, other)


def stack_kernel(count, blocks, basis, clip_mask, inv_var, out, model):
    epochs, rows, width = clip_mask.shape
    columns = width // CELL
    parts = rows // SUB
    depth = SUB * count
    lane = lax.broadcasted_iota(jnp.int32, (SUB, LANES), 1)
    line = lax.broadcasted_iota(jnp.int32, (SUB, LANES), 0)
    diagonal = (lane >= line * count) & (lane < (line + 1) * count)
    spread = []
    for e in range(epochs):
        tail = blocks[e, columns * rows :, :].astype(jnp.float32)[:SUB]
        terms = []
        for term in range(3):
            value = tail if term == 0 else pltpu.roll(tail, LANES - term * count, 1)
            value = jnp.where(lane < count, value, 0.0)
            step = count
            while step < LANES:
                value = value + pltpu.roll(value, step, 1)
                step *= 2
            terms.append(value)
        spread.append(terms)
    for c in range(columns):
        at = slice(c * CELL, (c + 1) * CELL)
        weights = jnp.concatenate(
            [
                jnp.concatenate(
                    [
                        jnp.where(
                            diagonal,
                            jnp.broadcast_to(spread[e][term][c : c + 1], (SUB, LANES)),
                            0.0,
                        )
                        for e in range(epochs)
                    ],
                    axis=0,
                ).astype(jnp.bfloat16)
                for term in range(3)
            ],
            axis=1,
        )
        planes = jnp.concatenate(
            [basis[p * depth : (p + 1) * depth, at] for p in range(parts)], axis=1
        )
        model[...] = jnp.dot(
            weights, jnp.concatenate([planes] * 3, axis=0), preferred_element_type=jnp.float32
        )
        for p in range(parts):
            top = slice(p * SUB, (p + 1) * SUB)
            values, weight_iv, base = [], [], []
            for e in range(epochs):
                science = blocks[e, c * rows : (c + 1) * rows, :].astype(jnp.float32)[top]
                difference = science - model[e * SUB : (e + 1) * SUB, p * CELL : (p + 1) * CELL]
                values.append(difference.astype(jnp.bfloat16).astype(jnp.float32))
                iv = inv_var[e, :, at].astype(jnp.float32)[top]
                weight_iv.append(iv)
                base.append(clip_mask[e, top, at].astype(jnp.float32) * iv)
            num = tree_sum(b * v for b, v in zip(base, values))
            den = tree_sum(base)
            mean = num / (1.0 + den)
            for sweep in range(ITERS):
                weight = []
                for e in range(epochs):
                    resid = values[e] - mean
                    weight.append(base[e] / (1.0 + weight_iv[e] * resid * resid))
                num = tree_sum(w * v for w, v in zip(weight, values))
                den = tree_sum(weight)
                mean = num / (1.0 + den)
            out[top, at] = num / jnp.sqrt(1.0 + den)


def stack(count, blocks, basis, clip_mask, inv_var):
    epochs, rows, width = clip_mask.shape
    return pl.pallas_call(
        functools.partial(stack_kernel, count),
        out_shape=jax.ShapeDtypeStruct((rows, width), jnp.float32),
        scratch_shapes=[pltpu.VMEM((epochs * SUB, rows // SUB * CELL), jnp.float32)],
        compiler_params=pltpu.CompilerParams(vmem_limit_bytes=VMEM_LIMIT),
        cost_estimate=pl.CostEstimate(
            flops=100 * epochs * rows * width, bytes_accessed=10**6, transcendentals=0
        ),
    )(blocks, basis, clip_mask, inv_var)


def local(science, template, kernels, coef, grid_index, clip_mask, inv_var):
    rows = template.shape[0]
    count = lax.axis_size("epoch")
    blocks = pack(science, coef, grid_index, rows)
    blocks = lax.all_to_all(blocks, "epoch", split_axis=0, concat_axis=0, tiled=True)
    pair = lax.ppermute(template, "epoch", [(i, i ^ 1) for i in range(count)])
    swap = [(i, i + 1) for i in range(1, count - 1, 2)]
    other = lax.ppermute(template, "epoch", swap + [(b, a) for a, b in swap])
    basis = basis_rows(kernels, template, pair, other)
    return stack(kernels.shape[0], blocks, basis, clip_mask, inv_var)


def solution(mesh):
    return jax.shard_map(
        local,
        mesh=mesh,
        in_specs=(
            P(("groups", "epoch"), None, None),
            P(("groups", "epoch"), None),
            P(),
            P(("groups", "epoch"), None, None),
            P(("groups", "epoch"), None, None),
            P("groups", "epoch", None),
            P("groups", "epoch", None),
        ),
        out_specs=P(("groups", "epoch"), None),
        check_vma=False,
    )
```

```python
import functools

import jax
import jax.numpy as jnp
from jax import lax
from jax.experimental import pallas as pl
from jax.experimental.pallas import tpu as pltpu
from jax.sharding import PartitionSpec as P

CELL = 128
ITERS = 3
LANES = 128
SUB = 8
TILE = 16
VMEM_LIMIT = 16 * 1024 * 1024


def up(value, unit):
    return -(-value // unit) * unit


def tree_sum(items):
    items = list(items)
    while len(items) > 1:
        items = [
            items[i] + items[i + 1] if i + 1 < len(items) else items[i]
            for i in range(0, len(items), 2)
        ]
    return items[0]


def pack_kernel(fast, science, template, coef, grid_index, *refs):
    blocks = refs[:fast]
    spread, cells, sems, small = refs[fast:]
    rows, width = template.shape
    columns = width // CELL
    slow = science.shape[0]
    basis = coef.shape[1]
    here = lax.rem(lax.axis_index("epoch"), fast)
    cell_copy = pltpu.make_async_copy(grid_index, cells, small.at[0])
    coef_copy = pltpu.make_async_copy(coef, spread, small.at[1])
    cell_copy.start()
    coef_copy.start()
    moves = []
    for c in range(columns):
        at = slice(c * CELL, (c + 1) * CELL)
        for k in range(fast):
            moves.append(
                pltpu.make_async_copy(
                    science.at[:, here ^ k, :, at],
                    blocks[k].at[c * slow : (c + 1) * slow],
                    sems.at[k, c],
                )
            )
        moves.append(
            pltpu.make_async_copy(
                template.at[:, at], blocks[1].at[blocks[1].shape[0] - columns + c], small.at[2 + c]
            )
        )
    for move in moves:
        move.start()
    cell_copy.wait()
    coef_copy.wait()
    picked = [
        spread[pl.ds(cells[r, c], 1), :] for r in range(cells.shape[0]) for c in range(columns)
    ]
    size = up(len(picked), rows)
    if size > len(picked):
        picked.append(jnp.zeros((size - len(picked), basis), jnp.float32))
    table = jnp.concatenate(picked, axis=0)
    table = jnp.concatenate([table, jnp.zeros((size, LANES - basis), jnp.float32)], axis=1)
    first = table.astype(jnp.bfloat16).astype(jnp.float32)
    rest = table - first
    second = rest.astype(jnp.bfloat16).astype(jnp.float32)
    third = rest - second
    table = first + pltpu.roll(second, basis, 1) + pltpu.roll(third, 2 * basis, 1)
    table = table.astype(jnp.bfloat16)
    for k in range(fast):
        for g in range(size // rows):
            blocks[k][columns * slow + g] = table[g * rows : (g + 1) * rows]
    for move in moves:
        move.wait()


def pack(science, template, coef, grid_index, fast):
    rows, width = template.shape
    slow = science.shape[1] // rows // fast
    columns = width // CELL
    groups = slow * columns + up(grid_index.shape[1] * columns, rows) // rows
    shapes = [
        jax.ShapeDtypeStruct(
            (groups + (columns if k == 1 else 0), rows, LANES), jnp.bfloat16
        )
        for k in range(fast)
    ]
    return pl.pallas_call(
        functools.partial(pack_kernel, fast),
        out_shape=shapes,
        in_specs=[pl.BlockSpec(memory_space=pltpu.HBM)] * 4,
        out_specs=[pl.BlockSpec(memory_space=pltpu.VMEM)] * fast,
        scratch_shapes=[
            pltpu.VMEM(coef.shape[1:], jnp.float32),
            pltpu.SMEM(grid_index.shape[1:], jnp.int32),
            pltpu.SemaphoreType.DMA((fast, columns)),
            pltpu.SemaphoreType.DMA((2 + columns,)),
        ],
        compiler_params=pltpu.CompilerParams(vmem_limit_bytes=VMEM_LIMIT),
        cost_estimate=pl.CostEstimate(flops=0, bytes_accessed=500_000, transcendentals=0),
    )(science.reshape(slow, fast, rows, width), template, coef[0], grid_index[0])


def route_kernel(fast, slow, columns, *refs):
    held, sent, tails = refs[:fast], refs[fast : fast + slow], refs[fast + slow]
    rows = held[0].shape[1]
    me = lax.axis_index("epoch")
    across, here = lax.div(me, fast), lax.rem(me, fast)
    span = tails.shape[1] // rows
    for j in range(fast):
        for g in range(span):
            tails[j, g * rows : (g + 1) * rows] = held[j][columns * slow + g].astype(jnp.float32)
    for k in range(slow):
        to = across ^ k
        for j in range(fast):
            for c in range(columns):
                sent[k][j * columns + c] = held[j][c * slow + to]
        cell_row = lax.div((to * fast + here) * rows, CELL)
        picked = [
            tails[j, pl.ds(cell_row * columns + c, 1), :]
            for j in range(fast)
            for c in range(columns)
        ]
        size = up(len(picked), rows)
        if size > len(picked):
            picked.append(jnp.zeros((size - len(picked), LANES), jnp.float32))
        table = jnp.concatenate(picked, axis=0).astype(jnp.bfloat16)
        for g in range(size // rows):
            sent[k][fast * columns + g] = table[g * rows : (g + 1) * rows]


def route(held, slow, columns):
    fast = len(held)
    rows = held[0].shape[1]
    groups = fast * columns + up(fast * columns, rows) // rows
    tail = (held[0].shape[0] - slow * columns) * rows
    return pl.pallas_call(
        functools.partial(route_kernel, fast, slow, columns),
        out_shape=[jax.ShapeDtypeStruct((groups, rows, LANES), jnp.bfloat16)] * slow,
        scratch_shapes=[pltpu.VMEM((fast, tail, LANES), jnp.float32)],
        compiler_params=pltpu.CompilerParams(vmem_limit_bytes=VMEM_LIMIT),
        cost_estimate=pl.CostEstimate(flops=0, bytes_accessed=500_000, transcendentals=0),
    )(*held)


def basis_kernel(slot, kernels, own, pair, other, out, image, left, right):
    side, count, _ = kernels.shape
    half = side // 2
    rows, width = own.shape
    span = image.shape[1]
    odd = lax.rem(lax.axis_index("epoch"), 2) == 1
    image[...] = jnp.zeros(image.shape, jnp.float32)
    columns = width // CELL
    near = [pair[pair.shape[0] - columns + c].astype(jnp.float32) for c in range(columns)]
    near = jnp.concatenate(near, axis=1)
    far = other[...].astype(jnp.float32)
    low = jnp.where(odd, near, far)
    high = jnp.where(odd, far, near)
    image[:half, :width] = low[rows - half :, :]
    image[half : half + rows, :width] = own[...].astype(jnp.float32)
    image[half + rows : 2 * half + rows, :width] = high[:half, :]
    image[...] = pltpu.roll(image[...], (span + half + 1 - slot) % span, 1)
    flip = (
        lax.broadcasted_iota(jnp.int32, (side, LANES), 0)
        + lax.broadcasted_iota(jnp.int32, (side, LANES), 1)
        == slot - 1
    ).astype(jnp.float32).astype(jnp.bfloat16)
    per = LANES // slot
    lines = [
        jnp.dot(kernels[u], flip, preferred_element_type=jnp.float32) for u in range(side)
    ]
    left[...] = jnp.zeros(left.shape, jnp.bfloat16)
    for phase in range(min(per, rows)):
        chunks = {}
        for u in range(side):
            chunk, place = divmod(u + phase, per)
            line = lines[u] if place == 0 else pltpu.roll(lines[u], place * slot, 1)
            chunks[chunk] = line if chunk not in chunks else chunks[chunk] + line
        for y in range(phase, rows, per):
            for chunk, value in chunks.items():
                at = (y // per + chunk) * LANES
                left[y * count : (y + 1) * count, at : at + LANES] = value.astype(jnp.bfloat16)
    for row in range(rows + 2 * half):
        line = jnp.broadcast_to(image[row : row + 1, :], (slot, span))
        moved = pltpu.roll(line, 0, 1, stride=1, stride_axis=0)
        right[row * slot : (row + 1) * slot, :] = moved[:, :width].astype(jnp.bfloat16)
    out[...] = jnp.dot(
        left[...], right[...], preferred_element_type=jnp.float32
    ).astype(jnp.bfloat16)


def basis_rows(kernels, own, pair, other):
    count, side, _ = kernels.shape
    rows, width = own.shape
    slot = up(side, 32)
    lines = rows + side - 1
    span = up(width + side, LANES)
    depth = up(lines * slot, LANES)
    return pl.pallas_call(
        functools.partial(basis_kernel, slot),
        out_shape=jax.ShapeDtypeStruct((rows * count, width), jnp.bfloat16),
        scratch_shapes=[
            pltpu.VMEM((up(lines, SUB), span), jnp.float32),
            pltpu.VMEM((rows * count, depth), jnp.bfloat16),
            pltpu.VMEM((depth, width), jnp.bfloat16),
        ],
        compiler_params=pltpu.CompilerParams(vmem_limit_bytes=VMEM_LIMIT),
        cost_estimate=pl.CostEstimate(
            flops=2 * rows * count * depth * width, bytes_accessed=600_000, transcendentals=0
        ),
    )(kernels.transpose(1, 0, 2), own, pair, other)


def stack_kernel(count, fast, *refs):
    slow = len(refs) - 5
    blocks = refs[:slow]
    basis, clip_mask, inv_var, out, model = refs[slow:]
    epochs, rows, width = clip_mask.shape
    columns = width // CELL
    parts = rows // SUB
    depth = SUB * count
    lane = lax.broadcasted_iota(jnp.int32, (SUB, LANES), 1)
    line = lax.broadcasted_iota(jnp.int32, (SUB, LANES), 0)
    diagonal = (lane >= line * count) & (lane < (line + 1) * count)
    me = lax.axis_index("epoch")
    across, here = lax.div(me, fast), lax.rem(me, fast)
    order, spread = [], []
    for k in range(slow):
        tail = jnp.concatenate(
            [blocks[k][g].astype(jnp.float32) for g in range(fast * columns, blocks[k].shape[0])],
            axis=0,
        )
        own_lane = lax.broadcasted_iota(jnp.int32, tail.shape, 1) < count
        terms = []
        for term in range(3):
            value = tail if term == 0 else pltpu.roll(tail, LANES - term * count, 1)
            value = jnp.where(own_lane, value, 0.0)
            step = count
            while step < LANES:
                value = value + pltpu.roll(value, step, 1)
                step *= 2
            terms.append(value)
        for j in range(fast):
            order.append((k, j, (across ^ k) * fast + (here ^ j)))
            spread.append([value[j * columns : (j + 1) * columns] for value in terms])
    for c in range(columns):
        at = slice(c * CELL, (c + 1) * CELL)
        weights = jnp.concatenate(
            [
                jnp.concatenate(
                    [
                        jnp.where(
                            diagonal,
                            jnp.broadcast_to(spread[e][term][c : c + 1], (SUB, LANES)),
                            0.0,
                        )
                        for e in range(epochs)
                    ],
                    axis=0,
                ).astype(jnp.bfloat16)
                for term in range(3)
            ],
            axis=1,
        )
        planes = jnp.concatenate(
            [basis[p * depth : (p + 1) * depth, at] for p in range(parts)], axis=1
        )
        model[...] = jnp.dot(
            weights, jnp.concatenate([planes] * 3, axis=0), preferred_element_type=jnp.float32
        )
        for p in range(parts):
            top = slice(p * SUB, (p + 1) * SUB)
            values, weight_iv, base = [], [], []
            for e in range(epochs):
                k, j, epoch = order[e]
                science = blocks[k][j * columns + c].astype(jnp.float32)[top]
                difference = science - model[e * SUB : (e + 1) * SUB, p * CELL : (p + 1) * CELL]
                values.append(difference.astype(jnp.bfloat16).astype(jnp.float32))
                iv = inv_var[epoch, :, at].astype(jnp.float32)[top]
                weight_iv.append(iv)
                base.append(clip_mask[epoch, top, at].astype(jnp.float32) * iv)
            num = tree_sum(b * v for b, v in zip(base, values))
            den = tree_sum(base)
            mean = num / (1.0 + den)
            for sweep in range(ITERS):
                weight = []
                for e in range(epochs):
                    resid = values[e] - mean
                    weight.append(base[e] / (1.0 + weight_iv[e] * resid * resid))
                num = tree_sum(w * v for w, v in zip(weight, values))
                den = tree_sum(weight)
                mean = num / (1.0 + den)
            out[top, at] = num / jnp.sqrt(1.0 + den)


def stack(count, fast, blocks, basis, clip_mask, inv_var):
    epochs, rows, width = clip_mask.shape
    return pl.pallas_call(
        functools.partial(stack_kernel, count, fast),
        out_shape=jax.ShapeDtypeStruct((rows, width), jnp.float32),
        scratch_shapes=[pltpu.VMEM((epochs * SUB, rows // SUB * CELL), jnp.float32)],
        compiler_params=pltpu.CompilerParams(vmem_limit_bytes=VMEM_LIMIT),
        cost_estimate=pl.CostEstimate(
            flops=100 * epochs * rows * width, bytes_accessed=10**6, transcendentals=0
        ),
    )(*blocks, basis, clip_mask, inv_var)


def exchange(block, step):
    return lax.ppermute(block, "epoch", [(i, i ^ step) for i in range(lax.axis_size("epoch"))])


def local(science, template, kernels, coef, grid_index, clip_mask, inv_var):
    count = lax.axis_size("epoch")
    fast = 2
    while 4 * fast * fast <= count:
        fast *= 2
    slow = count // fast
    columns = template.shape[1] // CELL
    sent = pack(science, template, coef, grid_index, fast)
    held = [sent[0]] + [exchange(sent[k], k) for k in range(1, fast)]
    swap = [(i, i + 1) for i in range(1, count - 1, 2)]
    other = lax.ppermute(template, "epoch", swap + [(b, a) for a, b in swap])
    sent = route(held, slow, columns)
    blocks = [sent[0]] + [exchange(sent[k], k * fast) for k in range(1, slow)]
    basis = basis_rows(kernels, template, held[1], other)
    return stack(kernels.shape[0], fast, blocks, basis, clip_mask, inv_var)


def solution(mesh):
    return jax.shard_map(
        local,
        mesh=mesh,
        in_specs=(
            P(("groups", "epoch"), None, None),
            P(("groups", "epoch"), None),
            P(),
            P(("groups", "epoch"), None, None),
            P(("groups", "epoch"), None, None),
            P("groups", "epoch", None),
            P("groups", "epoch", None),
        ),
        out_specs=P(("groups", "epoch"), None),
        check_vma=False,
    )
```

```python
import functools

import jax
import jax.numpy as jnp
from jax import lax
from jax.experimental import pallas as pl
from jax.experimental.pallas import tpu as pltpu
from jax.sharding import PartitionSpec as P

CELL = 128
ITERS = 3
LANES = 128
SUB = 8
TILE = 16
VMEM_LIMIT = 16 * 1024 * 1024


def up(value, unit):
    return -(-value // unit) * unit


def tree_sum(items):
    items = list(items)
    while len(items) > 1:
        items = [
            items[i] + items[i + 1] if i + 1 < len(items) else items[i]
            for i in range(0, len(items), 2)
        ]
    return items[0]


def cell_rows(coef, grid_index):
    levels, basis = coef.shape
    level = lax.broadcasted_iota(jnp.int32, (levels, basis), 0)
    picked = []
    for r in range(grid_index.shape[0]):
        for c in range(grid_index.shape[1]):
            chosen = jnp.broadcast_to(grid_index[r : r + 1, c : c + 1], (levels, basis)) == level
            picked.append(jnp.sum(jnp.where(chosen, coef[...], 0.0), axis=0, keepdims=True))
    table = jnp.concatenate(picked, axis=0)
    table = jnp.concatenate(
        [table, jnp.zeros((table.shape[0], LANES - basis), jnp.float32)], axis=1
    )
    first = table.astype(jnp.bfloat16).astype(jnp.float32)
    rest = table - first
    second = rest.astype(jnp.bfloat16).astype(jnp.float32)
    third = rest - second
    return first + pltpu.roll(second, basis, 1) + pltpu.roll(third, 2 * basis, 1)


def fill_tail(block, at, tables):
    rows = block.shape[1]
    table = jnp.concatenate(tables, axis=0)
    size = up(table.shape[0], rows)
    if size > table.shape[0]:
        table = jnp.concatenate(
            [table, jnp.zeros((size - table.shape[0], LANES), jnp.float32)], axis=0
        )
    table = table.astype(jnp.bfloat16)
    for g in range(size // rows):
        block[at + g] = table[g * rows : (g + 1) * rows]


def stage_kernel(science, coef, grid_index, rows_out, table_out):
    slow, middle, cores, _, _ = science.shape
    core = lax.rem(lax.axis_index("epoch"), cores)
    for z in range(slow):
        for k in range(middle):
            rows_out[z, k] = science[z, k, core]
    table_out[...] = cell_rows(coef, grid_index)


def stage(science, coef, grid_index):
    slow, middle, _, rows, width = science.shape
    cells = grid_index.shape[0] * grid_index.shape[1]
    return pl.pallas_call(
        stage_kernel,
        out_shape=[
            jax.ShapeDtypeStruct((slow, middle, rows, width), jnp.bfloat16),
            jax.ShapeDtypeStruct((cells, LANES), jnp.float32),
        ],
        compiler_params=pltpu.CompilerParams(vmem_limit_bytes=VMEM_LIMIT),
        cost_estimate=pl.CostEstimate(flops=0, bytes_accessed=1_000_000, transcendentals=0),
    )(science, coef, grid_index)


def pack_kernel(own, pair, own_table, pair_coef, pair_index, after, *blocks):
    slow, middle, cores, rows, width = pair.shape
    columns = width // CELL
    me = lax.axis_index("epoch")
    core, here = lax.rem(me, cores), lax.rem(lax.div(me, cores), middle)
    tables = [own_table[...], cell_rows(pair_coef, pair_index)]
    for k in range(middle):
        to = here ^ k
        for c in range(columns):
            at = slice(c * CELL, (c + 1) * CELL)
            for z in range(slow):
                blocks[k][c * slow + z] = own[z, to, :, at]
                blocks[k][(columns + c) * slow + z] = pair[z, to, core, :, at]
        fill_tail(blocks[k], cores * columns * slow, tables)


def pack(own, pair, own_table, pair_coef, pair_index, after):
    slow, middle, cores, rows, width = pair.shape
    columns = width // CELL
    groups = cores * slow * columns + up(cores * own_table.shape[0], rows) // rows
    return pl.pallas_call(
        pack_kernel,
        out_shape=[jax.ShapeDtypeStruct((groups, rows, LANES), jnp.bfloat16)] * middle,
        compiler_params=pltpu.CompilerParams(vmem_limit_bytes=VMEM_LIMIT),
        cost_estimate=pl.CostEstimate(flops=0, bytes_accessed=500_000, transcendentals=0),
    )(own, pair, own_table, pair_coef, pair_index, after)


def route_kernel(middle, slow, columns, cells, *refs):
    held, sent, tails = refs[:middle], refs[middle + 1 : middle + 1 + slow], refs[-1]
    rows = held[0].shape[1]
    me = lax.axis_index("epoch")
    across, here = lax.div(me, 2 * middle), lax.rem(me, 2 * middle)
    span = tails.shape[1] // rows
    tail = 2 * columns * slow
    for j in range(middle):
        for g in range(span):
            tails[j, g * rows : (g + 1) * rows] = held[j][tail + g].astype(jnp.float32)
    for k in range(slow):
        to = across ^ k
        for j in range(middle):
            for g in range(2 * columns):
                sent[k][j * 2 * columns + g] = held[j][g * slow + to]
        cell_row = lax.div((to * 2 * middle + here) * rows, CELL)
        picked = [
            tails[j, pl.ds(q * cells + cell_row * columns + c, 1), :]
            for j in range(middle)
            for q in range(2)
            for c in range(columns)
        ]
        fill_tail(sent[k], 2 * middle * columns, picked)


def route(held, after, slow, columns, cells):
    middle = len(held)
    rows = held[0].shape[1]
    groups = 2 * middle * columns + up(2 * middle * columns, rows) // rows
    tail = (held[0].shape[0] - 2 * slow * columns) * rows
    return pl.pallas_call(
        functools.partial(route_kernel, middle, slow, columns, cells),
        out_shape=[jax.ShapeDtypeStruct((groups, rows, LANES), jnp.bfloat16)] * slow,
        scratch_shapes=[pltpu.VMEM((middle, tail, LANES), jnp.float32)],
        compiler_params=pltpu.CompilerParams(vmem_limit_bytes=VMEM_LIMIT),
        cost_estimate=pl.CostEstimate(flops=0, bytes_accessed=500_000, transcendentals=0),
    )(*held, after)


def basis_kernel(slot, kernels, own, pair, other, out, image, left, right):
    side, count, _ = kernels.shape
    half = side // 2
    rows, width = own.shape
    span = image.shape[1]
    odd = lax.rem(lax.axis_index("epoch"), 2) == 1
    image[...] = jnp.zeros(image.shape, jnp.float32)
    near = pair[...].astype(jnp.float32)
    far = other[...].astype(jnp.float32)
    low = jnp.where(odd, near, far)
    high = jnp.where(odd, far, near)
    image[:half, :width] = low[rows - half :, :]
    image[half : half + rows, :width] = own[...].astype(jnp.float32)
    image[half + rows : 2 * half + rows, :width] = high[:half, :]
    image[...] = pltpu.roll(image[...], (span + half + 1 - slot) % span, 1)
    flip = (
        lax.broadcasted_iota(jnp.int32, (side, LANES), 0)
        + lax.broadcasted_iota(jnp.int32, (side, LANES), 1)
        == slot - 1
    ).astype(jnp.float32).astype(jnp.bfloat16)
    per = LANES // slot
    lines = [
        jnp.dot(kernels[u], flip, preferred_element_type=jnp.float32) for u in range(side)
    ]
    left[...] = jnp.zeros(left.shape, jnp.bfloat16)
    for phase in range(min(per, rows)):
        chunks = {}
        for u in range(side):
            chunk, place = divmod(u + phase, per)
            line = lines[u] if place == 0 else pltpu.roll(lines[u], place * slot, 1)
            chunks[chunk] = line if chunk not in chunks else chunks[chunk] + line
        for y in range(phase, rows, per):
            for chunk, value in chunks.items():
                at = (y // per + chunk) * LANES
                left[y * count : (y + 1) * count, at : at + LANES] = value.astype(jnp.bfloat16)
    for row in range(rows + 2 * half):
        line = jnp.broadcast_to(image[row : row + 1, :], (slot, span))
        moved = pltpu.roll(line, 0, 1, stride=1, stride_axis=0)
        right[row * slot : (row + 1) * slot, :] = moved[:, :width].astype(jnp.bfloat16)
    out[...] = jnp.dot(
        left[...], right[...], preferred_element_type=jnp.float32
    ).astype(jnp.bfloat16)


def basis_rows(kernels, own, pair, other):
    count, side, _ = kernels.shape
    rows, width = own.shape
    slot = up(side, 32)
    lines = rows + side - 1
    span = up(width + side, LANES)
    depth = up(lines * slot, LANES)
    return pl.pallas_call(
        functools.partial(basis_kernel, slot),
        out_shape=jax.ShapeDtypeStruct((rows * count, width), jnp.bfloat16),
        scratch_shapes=[
            pltpu.VMEM((up(lines, SUB), span), jnp.float32),
            pltpu.VMEM((rows * count, depth), jnp.bfloat16),
            pltpu.VMEM((depth, width), jnp.bfloat16),
        ],
        compiler_params=pltpu.CompilerParams(vmem_limit_bytes=VMEM_LIMIT),
        cost_estimate=pl.CostEstimate(
            flops=2 * rows * count * depth * width, bytes_accessed=600_000, transcendentals=0
        ),
    )(kernels.transpose(1, 0, 2), own, pair, other)


def stack_kernel(count, units, *refs):
    slow = len(refs) - 5
    blocks = refs[:slow]
    basis, clip_mask, inv_var, out, model = refs[slow:]
    epochs, rows, width = clip_mask.shape
    columns = width // CELL
    parts = rows // SUB
    depth = SUB * count
    lane = lax.broadcasted_iota(jnp.int32, (SUB, LANES), 1)
    line = lax.broadcasted_iota(jnp.int32, (SUB, LANES), 0)
    diagonal = (lane >= line * count) & (lane < (line + 1) * count)
    me = lax.axis_index("epoch")
    order, spread = [], []
    for k in range(slow):
        tail = jnp.concatenate(
            [blocks[k][g].astype(jnp.float32) for g in range(units * columns, blocks[k].shape[0])],
            axis=0,
        )
        own_lane = lax.broadcasted_iota(jnp.int32, tail.shape, 1) < count
        terms = []
        for term in range(3):
            value = tail if term == 0 else pltpu.roll(tail, LANES - term * count, 1)
            value = jnp.where(own_lane, value, 0.0)
            step = count
            while step < LANES:
                value = value + pltpu.roll(value, step, 1)
                step *= 2
            terms.append(value)
        for j in range(units):
            order.append((k, j, me ^ (k * units + j)))
            spread.append([value[j * columns : (j + 1) * columns] for value in terms])
    for c in range(columns):
        at = slice(c * CELL, (c + 1) * CELL)
        weights = jnp.concatenate(
            [
                jnp.concatenate(
                    [
                        jnp.where(
                            diagonal,
                            jnp.broadcast_to(spread[e][term][c : c + 1], (SUB, LANES)),
                            0.0,
                        )
                        for e in range(epochs)
                    ],
                    axis=0,
                ).astype(jnp.bfloat16)
                for term in range(3)
            ],
            axis=1,
        )
        planes = jnp.concatenate(
            [basis[p * depth : (p + 1) * depth, at] for p in range(parts)], axis=1
        )
        model[...] = jnp.dot(
            weights, jnp.concatenate([planes] * 3, axis=0), preferred_element_type=jnp.float32
        )
        for p in range(parts):
            top = slice(p * SUB, (p + 1) * SUB)
            values, weight_iv, base = [], [], []
            for e in range(epochs):
                k, j, epoch = order[e]
                science = blocks[k][j * columns + c].astype(jnp.float32)[top]
                difference = science - model[e * SUB : (e + 1) * SUB, p * CELL : (p + 1) * CELL]
                values.append(difference.astype(jnp.bfloat16).astype(jnp.float32))
                iv = inv_var[epoch, :, at].astype(jnp.float32)[top]
                weight_iv.append(iv)
                base.append(clip_mask[epoch, top, at].astype(jnp.float32) * iv)
            num = tree_sum(b * v for b, v in zip(base, values))
            den = tree_sum(base)
            mean = num / (1.0 + den)
            for sweep in range(ITERS):
                weight = []
                for e in range(epochs):
                    resid = values[e] - mean
                    weight.append(base[e] / (1.0 + weight_iv[e] * resid * resid))
                num = tree_sum(w * v for w, v in zip(weight, values))
                den = tree_sum(weight)
                mean = num / (1.0 + den)
            out[top, at] = num / jnp.sqrt(1.0 + den)


def stack(count, units, blocks, basis, clip_mask, inv_var):
    epochs, rows, width = clip_mask.shape
    return pl.pallas_call(
        functools.partial(stack_kernel, count, units),
        out_shape=jax.ShapeDtypeStruct((rows, width), jnp.float32),
        scratch_shapes=[pltpu.VMEM((epochs * SUB, rows // SUB * CELL), jnp.float32)],
        compiler_params=pltpu.CompilerParams(vmem_limit_bytes=VMEM_LIMIT),
        cost_estimate=pl.CostEstimate(
            flops=100 * epochs * rows * width, bytes_accessed=10**6, transcendentals=0
        ),
    )(*blocks, basis, clip_mask, inv_var)


def exchange(block, step):
    return lax.ppermute(block, "epoch", [(i, i ^ step) for i in range(lax.axis_size("epoch"))])


def local(science, template, kernels, coef, grid_index, clip_mask, inv_var):
    count = lax.axis_size("epoch")
    rows, width = template.shape
    columns = width // CELL
    slow = 1
    while slow * slow * 2 < count:
        slow *= 2
    middle = count // 2 // slow
    units = 2 * middle
    view = (slow, middle, 2, rows, width)
    pair_science = exchange(science, 1).reshape(view)
    pair_coef = exchange(coef, 1)[0]
    pair_index = exchange(grid_index, 1)[0]
    pair = exchange(template, 1)
    own, table = stage(science.reshape(view), coef[0], grid_index[0])
    sent = pack(own, pair_science, table, pair_coef, pair_index, pair)
    held = [sent[0]] + [exchange(sent[k], 2 * k) for k in range(1, middle)]
    up_down = [(i, i + 2) if i % 2 == 0 else (i + 2, i) for i in range(count - 2)]
    other = lax.ppermute(pair, "epoch", up_down)
    sent = route(held, other, slow, columns, grid_index.shape[1] * columns)
    blocks = [sent[0]] + [exchange(sent[k], k * units) for k in range(1, slow)]
    basis = basis_rows(kernels, template, pair, other)
    return stack(kernels.shape[0], units, blocks, basis, clip_mask, inv_var)


def solution(mesh):
    return jax.shard_map(
        local,
        mesh=mesh,
        in_specs=(
            P(("groups", "epoch"), None, None),
            P(("groups", "epoch"), None),
            P(),
            P(("groups", "epoch"), None, None),
            P(("groups", "epoch"), None, None),
            P("groups", "epoch", None),
            P("groups", "epoch", None),
        ),
        out_specs=P(("groups", "epoch"), None),
        check_vma=False,
    )
```

```python
import functools

import jax
import jax.numpy as jnp
from jax import lax
from jax.experimental import pallas as pl
from jax.experimental.pallas import tpu as pltpu
from jax.sharding import PartitionSpec as P

CELL = 128
ITERS = 3
LANES = 128
SUB = 8
TILE = 16
VMEM_LIMIT = 16 * 1024 * 1024
ORDER = [7, 3, 1, 6, 5, 4, 2]


def up(value, unit):
    return -(-value // unit) * unit


def tree_sum(items):
    items = list(items)
    while len(items) > 1:
        items = [
            items[i] + items[i + 1] if i + 1 < len(items) else items[i]
            for i in range(0, len(items), 2)
        ]
    return items[0]


def cell_rows(coef, grid_index):
    levels, basis = coef.shape
    level = lax.broadcasted_iota(jnp.int32, (levels, basis), 0)
    picked = []
    for r in range(grid_index.shape[0]):
        for c in range(grid_index.shape[1]):
            chosen = jnp.broadcast_to(grid_index[r : r + 1, c : c + 1], (levels, basis)) == level
            picked.append(jnp.sum(jnp.where(chosen, coef[...], 0.0), axis=0, keepdims=True))
    table = jnp.concatenate(picked, axis=0)
    table = jnp.concatenate(
        [table, jnp.zeros((table.shape[0], LANES - basis), jnp.float32)], axis=1
    )
    first = table.astype(jnp.bfloat16).astype(jnp.float32)
    rest = table - first
    second = rest.astype(jnp.bfloat16).astype(jnp.float32)
    third = rest - second
    return first + pltpu.roll(second, basis, 1) + pltpu.roll(third, 2 * basis, 1)


def fill_tail(block, at, tables):
    rows = block.shape[1]
    table = jnp.concatenate(tables, axis=0)
    size = up(table.shape[0], rows)
    if size > table.shape[0]:
        table = jnp.concatenate(
            [table, jnp.zeros((size - table.shape[0], LANES), jnp.float32)], axis=0
        )
    table = table.astype(jnp.bfloat16)
    for g in range(size // rows):
        block[at + g] = table[g * rows : (g + 1) * rows]


def with_template(k):
    return k & (k + 1) == 0 and k > 0


def stage_kernel(science, coef, grid_index, out, table):
    core = lax.rem(lax.axis_index("epoch"), 2)
    for chip in range(science.shape[0]):
        out[chip] = science[chip, core]
    table[...] = cell_rows(coef, grid_index)


def stage(science, coef, grid_index):
    chips, _, rows, width = science.shape
    return pl.pallas_call(
        stage_kernel,
        out_shape=[
            jax.ShapeDtypeStruct((chips, rows, width), jnp.bfloat16),
            jax.ShapeDtypeStruct((grid_index.shape[0] * grid_index.shape[1], LANES), jnp.float32),
        ],
        compiler_params=pltpu.CompilerParams(vmem_limit_bytes=VMEM_LIMIT),
        cost_estimate=pl.CostEstimate(flops=0, bytes_accessed=1_000_000, transcendentals=0),
    )(science, coef, grid_index)


def pack_kernel(steps, own, pair, own_table, pair_coef, pair_index, template, *refs):
    blocks, tables = refs[:-1], refs[-1]
    rows, width = template.shape
    columns = width // CELL
    me = lax.axis_index("epoch")
    core, here = lax.rem(me, 2), lax.div(me, 2)
    half = tables.shape[0] // 2
    cells = own_table.shape[0]
    tables[:cells] = own_table[...]
    tables[half : half + cells] = cell_rows(pair_coef, pair_index)
    for k, block in zip(steps, blocks):
        to = here ^ k
        for c in range(columns):
            at = slice(c * CELL, (c + 1) * CELL)
            block[c] = own[to, :, at]
            block[columns + c] = pair[to, core, :, at]
            if with_template(k):
                block[block.shape[0] - columns + c] = template[:, at]
        cell_row = lax.div((to * 2 + core) * rows, CELL)
        picked = [
            tables[pl.ds(q * half + cell_row * columns + c, 1), :]
            for q in range(2)
            for c in range(columns)
        ]
        fill_tail(block, 2 * columns, picked)


def pack(own, pair, own_table, pair_coef, pair_index, template, steps):
    rows, width = template.shape
    columns = width // CELL
    groups = 2 * columns + up(2 * columns, rows) // rows
    half = up(own_table.shape[0], SUB)
    return pl.pallas_call(
        functools.partial(pack_kernel, steps),
        out_shape=[
            jax.ShapeDtypeStruct(
                (groups + (columns if with_template(k) else 0), rows, LANES), jnp.bfloat16
            )
            for k in steps
        ],
        scratch_shapes=[pltpu.VMEM((2 * half, LANES), jnp.float32)],
        compiler_params=pltpu.CompilerParams(vmem_limit_bytes=VMEM_LIMIT),
        cost_estimate=pl.CostEstimate(flops=0, bytes_accessed=500_000, transcendentals=0),
    )(own, pair, own_table, pair_coef, pair_index, template)


def basis_kernel(slot, steps, kernels, own, pair, *refs):
    held, (out, image, left, right) = refs[:-4], refs[-4:]
    side, count, _ = kernels.shape
    half = side // 2
    rows, width = own.shape
    columns = width // CELL
    span = image.shape[1]
    me = lax.axis_index("epoch")
    odd, here = lax.rem(me, 2) == 1, lax.div(me, 2)
    want = jnp.where(odd, here + 1, here - 1)
    image[...] = jnp.zeros(image.shape, jnp.float32)
    near = pair[...].astype(jnp.float32)
    far = jnp.zeros(own.shape, jnp.float32)
    for k, block in zip(steps, held):
        at = block.shape[0] - columns
        lines = [block[at + c].astype(jnp.float32) for c in range(columns)]
        far = jnp.where(here ^ k == want, jnp.concatenate(lines, axis=1), far)
    low = jnp.where(odd, near, far)
    high = jnp.where(odd, far, near)
    image[:half, :width] = low[rows - half :, :]
    image[half : half + rows, :width] = own[...].astype(jnp.float32)
    image[half + rows : 2 * half + rows, :width] = high[:half, :]
    image[...] = pltpu.roll(image[...], (span + half + 1 - slot) % span, 1)
    flip = (
        lax.broadcasted_iota(jnp.int32, (side, LANES), 0)
        + lax.broadcasted_iota(jnp.int32, (side, LANES), 1)
        == slot - 1
    ).astype(jnp.float32).astype(jnp.bfloat16)
    per = LANES // slot
    lines = [
        jnp.dot(kernels[u], flip, preferred_element_type=jnp.float32) for u in range(side)
    ]
    left[...] = jnp.zeros(left.shape, jnp.bfloat16)
    for phase in range(min(per, rows)):
        chunks = {}
        for u in range(side):
            chunk, place = divmod(u + phase, per)
            line = lines[u] if place == 0 else pltpu.roll(lines[u], place * slot, 1)
            chunks[chunk] = line if chunk not in chunks else chunks[chunk] + line
        for y in range(phase, rows, per):
            for chunk, value in chunks.items():
                at = (y // per + chunk) * LANES
                left[y * count : (y + 1) * count, at : at + LANES] = value.astype(jnp.bfloat16)
    for row in range(rows + 2 * half):
        line = jnp.broadcast_to(image[row : row + 1, :], (slot, span))
        moved = pltpu.roll(line, 0, 1, stride=1, stride_axis=0)
        right[row * slot : (row + 1) * slot, :] = moved[:, :width].astype(jnp.bfloat16)
    out[...] = jnp.dot(
        left[...], right[...], preferred_element_type=jnp.float32
    ).astype(jnp.bfloat16)


def basis_rows(kernels, own, pair, held, steps):
    count, side, _ = kernels.shape
    rows, width = own.shape
    slot = up(side, 32)
    lines = rows + side - 1
    span = up(width + side, LANES)
    depth = up(lines * slot, LANES)
    return pl.pallas_call(
        functools.partial(basis_kernel, slot, steps),
        out_shape=jax.ShapeDtypeStruct((rows * count, width), jnp.bfloat16),
        scratch_shapes=[
            pltpu.VMEM((up(lines, SUB), span), jnp.float32),
            pltpu.VMEM((rows * count, depth), jnp.bfloat16),
            pltpu.VMEM((depth, width), jnp.bfloat16),
        ],
        compiler_params=pltpu.CompilerParams(vmem_limit_bytes=VMEM_LIMIT),
        cost_estimate=pl.CostEstimate(
            flops=2 * rows * count * depth * width, bytes_accessed=600_000, transcendentals=0
        ),
    )(kernels.transpose(1, 0, 2), own, pair, *held)


def stack_kernel(count, steps, *refs):
    blocks = refs[:-5]
    basis, clip_mask, inv_var, out, model = refs[-5:]
    units = 2
    epochs, rows, width = clip_mask.shape
    columns = width // CELL
    parts = rows // SUB
    depth = SUB * count
    lane = lax.broadcasted_iota(jnp.int32, (SUB, LANES), 1)
    line = lax.broadcasted_iota(jnp.int32, (SUB, LANES), 0)
    diagonal = (lane >= line * count) & (lane < (line + 1) * count)
    me = lax.axis_index("epoch")
    order, spread = [], []
    for k, chip in enumerate(steps):
        span = up(units * columns, rows) // rows
        tail = [blocks[k][units * columns + g].astype(jnp.float32) for g in range(span)]
        tail = jnp.concatenate(tail, axis=0)
        own_lane = lax.broadcasted_iota(jnp.int32, tail.shape, 1) < count
        terms = []
        for term in range(3):
            value = tail if term == 0 else pltpu.roll(tail, LANES - term * count, 1)
            value = jnp.where(own_lane, value, 0.0)
            step = count
            while step < LANES:
                value = value + pltpu.roll(value, step, 1)
                step *= 2
            terms.append(value)
        for j in range(units):
            order.append((k, j, me ^ (chip * units + j)))
            spread.append([value[j * columns : (j + 1) * columns] for value in terms])
    for c in range(columns):
        at = slice(c * CELL, (c + 1) * CELL)
        weights = jnp.concatenate(
            [
                jnp.concatenate(
                    [
                        jnp.where(
                            diagonal,
                            jnp.broadcast_to(spread[e][term][c : c + 1], (SUB, LANES)),
                            0.0,
                        )
                        for e in range(epochs)
                    ],
                    axis=0,
                ).astype(jnp.bfloat16)
                for term in range(3)
            ],
            axis=1,
        )
        planes = jnp.concatenate(
            [basis[p * depth : (p + 1) * depth, at] for p in range(parts)], axis=1
        )
        model[...] = jnp.dot(
            weights, jnp.concatenate([planes] * 3, axis=0), preferred_element_type=jnp.float32
        )
        for p in range(parts):
            top = slice(p * SUB, (p + 1) * SUB)
            values, weight_iv, base = [], [], []
            for e in range(epochs):
                k, j, epoch = order[e]
                science = blocks[k][j * columns + c].astype(jnp.float32)[top]
                difference = science - model[e * SUB : (e + 1) * SUB, p * CELL : (p + 1) * CELL]
                values.append(difference.astype(jnp.bfloat16).astype(jnp.float32))
                iv = inv_var[epoch, :, at].astype(jnp.float32)[top]
                weight_iv.append(iv)
                base.append(clip_mask[epoch, top, at].astype(jnp.float32) * iv)
            num = tree_sum(b * v for b, v in zip(base, values))
            den = tree_sum(base)
            mean = num / (1.0 + den)
            for sweep in range(ITERS):
                weight = []
                for e in range(epochs):
                    resid = values[e] - mean
                    weight.append(base[e] / (1.0 + weight_iv[e] * resid * resid))
                num = tree_sum(w * v for w, v in zip(weight, values))
                den = tree_sum(weight)
                mean = num / (1.0 + den)
            out[top, at] = num / jnp.sqrt(1.0 + den)


def stack(count, steps, blocks, basis, clip_mask, inv_var):
    epochs, rows, width = clip_mask.shape
    return pl.pallas_call(
        functools.partial(stack_kernel, count, steps),
        out_shape=jax.ShapeDtypeStruct((rows, width), jnp.float32),
        scratch_shapes=[pltpu.VMEM((epochs * SUB, rows // SUB * CELL), jnp.float32)],
        compiler_params=pltpu.CompilerParams(vmem_limit_bytes=VMEM_LIMIT),
        cost_estimate=pl.CostEstimate(
            flops=100 * epochs * rows * width, bytes_accessed=10**6, transcendentals=0
        ),
    )(*blocks, basis, clip_mask, inv_var)


def exchange(block, step):
    return lax.ppermute(block, "epoch", [(i, i ^ step) for i in range(lax.axis_size("epoch"))])


def local(science, template, kernels, coef, grid_index, clip_mask, inv_var):
    rows, width = template.shape
    chips = lax.axis_size("epoch") // 2
    view = (chips, 2, rows, width)
    steps = [0] + ORDER + [k for k in range(1, chips) if k not in ORDER]
    pair_science = exchange(science, 1).reshape(view)
    pair_coef = exchange(coef, 1)[0]
    pair_index = exchange(grid_index, 1)[0]
    pair = exchange(template, 1)
    own, table = stage(science.reshape(view), coef[0], grid_index[0])
    sent = pack(own, pair_science, table, pair_coef, pair_index, pair, steps)
    blocks = [sent[0]] + [exchange(block, 2 * k) for block, k in zip(sent[1:], steps[1:])]
    near = [i for i, k in enumerate(steps) if with_template(k)]
    basis = basis_rows(
        kernels, template, pair, [blocks[i] for i in near], [steps[i] for i in near]
    )
    return stack(kernels.shape[0], steps, blocks, basis, clip_mask, inv_var)


def solution(mesh):
    return jax.shard_map(
        local,
        mesh=mesh,
        in_specs=(
            P(("groups", "epoch"), None, None),
            P(("groups", "epoch"), None),
            P(),
            P(("groups", "epoch"), None, None),
            P(("groups", "epoch"), None, None),
            P("groups", "epoch", None),
            P("groups", "epoch", None),
        ),
        out_specs=P(("groups", "epoch"), None),
        check_vma=False,
    )
```

```python
import functools

import jax
import jax.numpy as jnp
from jax import lax
from jax.experimental import pallas as pl
from jax.experimental.pallas import tpu as pltpu
from jax.sharding import PartitionSpec as P

CELL = 128
ITERS = 3
LANES = 128
SUB = 8
TILE = 16
VMEM_LIMIT = 16 * 1024 * 1024
ORDER = [7, 3, 1, 6, 5, 4, 2]


def up(value, unit):
    return -(-value // unit) * unit


def tree_sum(items):
    items = list(items)
    while len(items) > 1:
        items = [
            items[i] + items[i + 1] if i + 1 < len(items) else items[i]
            for i in range(0, len(items), 2)
        ]
    return items[0]


def cell_rows(coef, grid_index):
    levels, basis = coef.shape
    level = lax.broadcasted_iota(jnp.int32, (levels, basis), 0)
    picked = []
    for r in range(grid_index.shape[0]):
        for c in range(grid_index.shape[1]):
            chosen = jnp.broadcast_to(grid_index[r : r + 1, c : c + 1], (levels, basis)) == level
            picked.append(jnp.sum(jnp.where(chosen, coef[...], 0.0), axis=0, keepdims=True))
    table = jnp.concatenate(picked, axis=0)
    table = jnp.concatenate(
        [table, jnp.zeros((table.shape[0], LANES - basis), jnp.float32)], axis=1
    )
    first = table.astype(jnp.bfloat16).astype(jnp.float32)
    rest = table - first
    second = rest.astype(jnp.bfloat16).astype(jnp.float32)
    third = rest - second
    return first + pltpu.roll(second, basis, 1) + pltpu.roll(third, 2 * basis, 1)


def with_template(k):
    return k & (k + 1) == 0 and k > 0


def stage_kernel(science, coef, grid_index, first, out, table):
    core = lax.rem(lax.axis_index("epoch"), 2)
    for chip in range(science.shape[0]):
        out[chip] = science[chip, core]
    table[...] = cell_rows(coef, grid_index)


def nothing_kernel(out):
    out[...] = jnp.zeros(out.shape, jnp.float32)


def nothing():
    return pl.pallas_call(
        nothing_kernel,
        out_shape=jax.ShapeDtypeStruct((SUB, LANES), jnp.float32),
        compiler_params=pltpu.CompilerParams(vmem_limit_bytes=VMEM_LIMIT),
        cost_estimate=pl.CostEstimate(flops=1000000000, bytes_accessed=4096, transcendentals=0),
    )()


def stage(science, coef, grid_index, first):
    chips, _, rows, width = science.shape
    return pl.pallas_call(
        stage_kernel,
        out_shape=[
            jax.ShapeDtypeStruct((chips, rows, width), jnp.bfloat16),
            jax.ShapeDtypeStruct((grid_index.shape[0] * grid_index.shape[1], LANES), jnp.float32),
        ],
        compiler_params=pltpu.CompilerParams(vmem_limit_bytes=VMEM_LIMIT),
        cost_estimate=pl.CostEstimate(flops=0, bytes_accessed=1_000_000, transcendentals=0),
    )(science, coef, grid_index, first)


def pack_kernel(steps, own, pair, own_table, pair_coef, pair_index, template, *refs):
    blocks, tables = refs[:-1], refs[-1]
    rows, width = template.shape
    columns = width // CELL
    me = lax.axis_index("epoch")
    core, here = lax.rem(me, 2), lax.div(me, 2)
    half = tables.shape[0] // 2
    cells = own_table.shape[0]
    tables[:cells] = own_table[...]
    tables[half : half + cells] = cell_rows(pair_coef, pair_index)
    for k, block in zip(steps, blocks):
        to = here ^ k
        for c in range(columns):
            at = slice(c * CELL, (c + 1) * CELL)
            block[c * rows : (c + 1) * rows] = own[to, :, at]
            block[(columns + c) * rows : (columns + c + 1) * rows] = pair[to, core, :, at]
            if with_template(k):
                block[(2 * columns + c) * rows : (2 * columns + c + 1) * rows] = template[:, at]
        cell_row = lax.div((to * 2 + core) * rows, CELL)
        tail = [
            tables[pl.ds(q * half + cell_row * columns + c, 1), :]
            for q in range(2)
            for c in range(columns)
        ]
        tail.append(jnp.zeros((up(2 * columns, SUB) - 2 * columns, LANES), jnp.float32))
        block[block.shape[0] - up(2 * columns, SUB) :] = jnp.concatenate(
            [rows_ for rows_ in tail if rows_.shape[0]], axis=0
        ).astype(jnp.bfloat16)


def pack(own, pair, own_table, pair_coef, pair_index, template, steps):
    rows, width = template.shape
    columns = width // CELL
    tail = up(2 * columns, SUB)
    half = up(own_table.shape[0], SUB)
    return pl.pallas_call(
        functools.partial(pack_kernel, steps),
        out_shape=[
            jax.ShapeDtypeStruct(
                ((3 if with_template(k) else 2) * columns * rows + tail, LANES), jnp.bfloat16
            )
            for k in steps
        ],
        scratch_shapes=[pltpu.VMEM((2 * half, LANES), jnp.float32)],
        compiler_params=pltpu.CompilerParams(vmem_limit_bytes=VMEM_LIMIT),
        cost_estimate=pl.CostEstimate(flops=0, bytes_accessed=500_000, transcendentals=0),
    )(own, pair, own_table, pair_coef, pair_index, template)


def basis_kernel(slot, steps, kernels, own, pair, *refs):
    held, (out, image, left, right) = refs[:-4], refs[-4:]
    side, count, _ = kernels.shape
    half = side // 2
    rows, width = own.shape
    columns = width // CELL
    span = image.shape[1]
    me = lax.axis_index("epoch")
    odd, here = lax.rem(me, 2) == 1, lax.div(me, 2)
    want = jnp.where(odd, here + 1, here - 1)
    image[...] = jnp.zeros(image.shape, jnp.float32)
    near = pair[...].astype(jnp.float32)
    far = jnp.zeros(own.shape, jnp.float32)
    for k, block in zip(steps, held):
        at = 2 * columns * rows
        lines = [
            block[at + c * rows : at + (c + 1) * rows].astype(jnp.float32) for c in range(columns)
        ]
        far = jnp.where(here ^ k == want, jnp.concatenate(lines, axis=1), far)
    low = jnp.where(odd, near, far)
    high = jnp.where(odd, far, near)
    image[:half, :width] = low[rows - half :, :]
    image[half : half + rows, :width] = own[...].astype(jnp.float32)
    image[half + rows : 2 * half + rows, :width] = high[:half, :]
    image[...] = pltpu.roll(image[...], (span + half + 1 - slot) % span, 1)
    flip = (
        lax.broadcasted_iota(jnp.int32, (side, LANES), 0)
        + lax.broadcasted_iota(jnp.int32, (side, LANES), 1)
        == slot - 1
    ).astype(jnp.float32).astype(jnp.bfloat16)
    per = LANES // slot
    lines = [
        jnp.dot(kernels[u], flip, preferred_element_type=jnp.float32) for u in range(side)
    ]
    left[...] = jnp.zeros(left.shape, jnp.bfloat16)
    for phase in range(min(per, rows)):
        chunks = {}
        for u in range(side):
            chunk, place = divmod(u + phase, per)
            line = lines[u] if place == 0 else pltpu.roll(lines[u], place * slot, 1)
            chunks[chunk] = line if chunk not in chunks else chunks[chunk] + line
        for y in range(phase, rows, per):
            for chunk, value in chunks.items():
                at = (y // per + chunk) * LANES
                left[y * count : (y + 1) * count, at : at + LANES] = value.astype(jnp.bfloat16)
    for row in range(rows + 2 * half):
        line = jnp.broadcast_to(image[row : row + 1, :], (slot, span))
        moved = pltpu.roll(line, 0, 1, stride=1, stride_axis=0)
        right[row * slot : (row + 1) * slot, :] = moved[:, :width].astype(jnp.bfloat16)
    out[...] = jnp.dot(
        left[...], right[...], preferred_element_type=jnp.float32
    ).astype(jnp.bfloat16)


def basis_rows(kernels, own, pair, held, steps):
    count, side, _ = kernels.shape
    rows, width = own.shape
    slot = up(side, 32)
    lines = rows + side - 1
    span = up(width + side, LANES)
    depth = up(lines * slot, LANES)
    return pl.pallas_call(
        functools.partial(basis_kernel, slot, steps),
        out_shape=jax.ShapeDtypeStruct((rows * count, width), jnp.bfloat16),
        scratch_shapes=[
            pltpu.VMEM((up(lines, SUB), span), jnp.float32),
            pltpu.VMEM((rows * count, depth), jnp.bfloat16),
            pltpu.VMEM((depth, width), jnp.bfloat16),
        ],
        compiler_params=pltpu.CompilerParams(vmem_limit_bytes=VMEM_LIMIT),
        cost_estimate=pl.CostEstimate(
            flops=2 * rows * count * depth * width, bytes_accessed=600_000, transcendentals=0
        ),
    )(kernels.transpose(1, 0, 2), own, pair, *held)


def stack_kernel(count, steps, *refs):
    blocks = refs[:-5]
    basis, clip_mask, inv_var, out, model = refs[-5:]
    units = 2
    epochs, rows, width = clip_mask.shape
    columns = width // CELL
    parts = rows // SUB
    depth = SUB * count
    lane = lax.broadcasted_iota(jnp.int32, (SUB, LANES), 1)
    line = lax.broadcasted_iota(jnp.int32, (SUB, LANES), 0)
    diagonal = (lane >= line * count) & (lane < (line + 1) * count)
    me = lax.axis_index("epoch")
    order, spread = [], []
    for k, chip in enumerate(steps):
        size = up(units * columns, SUB)
        tail = blocks[k][blocks[k].shape[0] - size :].astype(jnp.float32)
        own_lane = lax.broadcasted_iota(jnp.int32, tail.shape, 1) < count
        terms = []
        for term in range(3):
            value = tail if term == 0 else pltpu.roll(tail, LANES - term * count, 1)
            value = jnp.where(own_lane, value, 0.0)
            step = count
            while step < LANES:
                value = value + pltpu.roll(value, step, 1)
                step *= 2
            terms.append(value)
        for j in range(units):
            order.append((k, j, me ^ (chip * units + j)))
            spread.append([value[j * columns : (j + 1) * columns] for value in terms])
    for c in range(columns):
        at = slice(c * CELL, (c + 1) * CELL)
        weights = jnp.concatenate(
            [
                jnp.concatenate(
                    [
                        jnp.where(
                            diagonal,
                            jnp.broadcast_to(spread[e][term][c : c + 1], (SUB, LANES)),
                            0.0,
                        )
                        for e in range(epochs)
                    ],
                    axis=0,
                ).astype(jnp.bfloat16)
                for term in range(3)
            ],
            axis=1,
        )
        planes = jnp.concatenate(
            [basis[p * depth : (p + 1) * depth, at] for p in range(parts)], axis=1
        )
        model[...] = jnp.dot(
            weights, jnp.concatenate([planes] * 3, axis=0), preferred_element_type=jnp.float32
        )
        for p in range(parts):
            top = slice(p * SUB, (p + 1) * SUB)
            values, weight_iv, base = [], [], []
            for e in range(epochs):
                k, j, epoch = order[e]
                first = (j * columns + c) * rows
                science = blocks[k][first : first + rows].astype(jnp.float32)[top]
                difference = science - model[e * SUB : (e + 1) * SUB, p * CELL : (p + 1) * CELL]
                values.append(difference.astype(jnp.bfloat16).astype(jnp.float32))
                iv = inv_var[epoch, :, at].astype(jnp.float32)[top]
                weight_iv.append(iv)
                base.append(clip_mask[epoch, top, at].astype(jnp.float32) * iv)
            num = tree_sum(b * v for b, v in zip(base, values))
            den = tree_sum(base)
            mean = num / (1.0 + den)
            for sweep in range(ITERS):
                weight = []
                for e in range(epochs):
                    resid = values[e] - mean
                    weight.append(base[e] / (1.0 + weight_iv[e] * resid * resid))
                num = tree_sum(w * v for w, v in zip(weight, values))
                den = tree_sum(weight)
                mean = num / (1.0 + den)
            out[top, at] = num / jnp.sqrt(1.0 + den)


def stack(count, steps, blocks, basis, clip_mask, inv_var):
    epochs, rows, width = clip_mask.shape
    return pl.pallas_call(
        functools.partial(stack_kernel, count, steps),
        out_shape=jax.ShapeDtypeStruct((rows, width), jnp.float32),
        scratch_shapes=[pltpu.VMEM((epochs * SUB, rows // SUB * CELL), jnp.float32)],
        compiler_params=pltpu.CompilerParams(vmem_limit_bytes=VMEM_LIMIT),
        cost_estimate=pl.CostEstimate(
            flops=100 * epochs * rows * width, bytes_accessed=10**6, transcendentals=0
        ),
    )(*blocks, basis, clip_mask, inv_var)


def exchange(block, step):
    return lax.ppermute(block, "epoch", [(i, i ^ step) for i in range(lax.axis_size("epoch"))])


def local(science, template, kernels, coef, grid_index, clip_mask, inv_var):
    rows, width = template.shape
    chips = lax.axis_size("epoch") // 2
    view = (chips, 2, rows, width)
    steps = [0] + ORDER + [k for k in range(1, chips) if k not in ORDER]
    pair_science = exchange(science, 1).reshape(view)
    pair_coef = exchange(coef, 1)[0]
    pair_index = exchange(grid_index, 1)[0]
    pair = exchange(template, 1)
    own, table = stage(science.reshape(view), coef[0], grid_index[0], nothing())
    sent = pack(own, pair_science, table, pair_coef, pair_index, pair, steps)
    blocks = [sent[0]] + [exchange(block, 2 * k) for block, k in zip(sent[1:], steps[1:])]
    near = [i for i, k in enumerate(steps) if with_template(k)]
    basis = basis_rows(
        kernels, template, pair, [blocks[i] for i in near], [steps[i] for i in near]
    )
    return stack(kernels.shape[0], steps, blocks, basis, clip_mask, inv_var)


def solution(mesh):
    return jax.shard_map(
        local,
        mesh=mesh,
        in_specs=(
            P(("groups", "epoch"), None, None),
            P(("groups", "epoch"), None),
            P(),
            P(("groups", "epoch"), None, None),
            P(("groups", "epoch"), None, None),
            P("groups", "epoch", None),
            P("groups", "epoch", None),
        ),
        out_specs=P(("groups", "epoch"), None),
        check_vma=False,
    )
```

```python
import functools

import jax
import jax.numpy as jnp
from jax import lax
from jax.experimental import pallas as pl
from jax.experimental.pallas import tpu as pltpu
from jax.sharding import PartitionSpec as P

CELL = 128
ITERS = 3
LANES = 128
SUB = 8
TILE = 16
VMEM_LIMIT = 16 * 1024 * 1024


def up(value, unit):
    return -(-value // unit) * unit


def tree_sum(items):
    items = list(items)
    while len(items) > 1:
        items = [
            items[i] + items[i + 1] if i + 1 < len(items) else items[i]
            for i in range(0, len(items), 2)
        ]
    return items[0]


def cell_rows(coef, grid_index):
    levels, basis = coef.shape
    level = lax.broadcasted_iota(jnp.int32, (levels, basis), 0)
    picked = []
    for r in range(grid_index.shape[0]):
        for c in range(grid_index.shape[1]):
            chosen = jnp.broadcast_to(grid_index[r : r + 1, c : c + 1], (levels, basis)) == level
            picked.append(jnp.sum(jnp.where(chosen, coef[...], 0.0), axis=0, keepdims=True))
    table = jnp.concatenate(picked, axis=0)
    table = jnp.concatenate(
        [table, jnp.zeros((table.shape[0], LANES - basis), jnp.float32)], axis=1
    )
    first = table.astype(jnp.bfloat16).astype(jnp.float32)
    rest = table - first
    second = rest.astype(jnp.bfloat16).astype(jnp.float32)
    third = rest - second
    return first + pltpu.roll(second, basis, 1) + pltpu.roll(third, 2 * basis, 1)


def with_template(k):
    return k & (k + 1) == 0 and k > 0


def handled(step, core):
    return step if isinstance(step, int) else jnp.where(core == 0, step[0], step[1])


def block_rows(step, rows, columns):
    cores = 1 if isinstance(step, int) else 2
    first = cores * 2 * columns * rows
    size = up(2 * columns, SUB)
    tail = first + (columns * rows if with_template(step if cores == 1 else step[0]) else 0)
    return first, tail, tail + size


def stage_kernel(science, template, coef, grid_index, first, out, edge, table):
    out[...] = science[...]
    edge[...] = template[...]
    table[...] = cell_rows(coef, grid_index)


def nothing_kernel(out):
    out[...] = jnp.zeros(out.shape, jnp.float32)


def nothing():
    return pl.pallas_call(
        nothing_kernel,
        out_shape=jax.ShapeDtypeStruct((SUB, LANES), jnp.float32),
        compiler_params=pltpu.CompilerParams(vmem_limit_bytes=VMEM_LIMIT),
        cost_estimate=pl.CostEstimate(flops=1000000000, bytes_accessed=4096, transcendentals=0),
    )()


def stage(science, template, coef, grid_index, first):
    chips, _, rows, width = science.shape
    return pl.pallas_call(
        stage_kernel,
        out_shape=[
            jax.ShapeDtypeStruct(science.shape, jnp.bfloat16),
            jax.ShapeDtypeStruct(template.shape, jnp.bfloat16),
            jax.ShapeDtypeStruct((grid_index.shape[0] * grid_index.shape[1], LANES), jnp.float32),
        ],
        compiler_params=pltpu.CompilerParams(vmem_limit_bytes=VMEM_LIMIT),
        cost_estimate=pl.CostEstimate(flops=0, bytes_accessed=1_000_000, transcendentals=0),
    )(science, template, coef, grid_index, first)


def pack_kernel(
    steps, own, pair, own_table, pair_coef, pair_index, own_template, pair_template, *refs
):
    blocks, tables = refs[:-1], refs[-1]
    rows, width = own_template.shape
    columns = width // CELL
    me = lax.axis_index("epoch")
    core, here = lax.rem(me, 2), lax.div(me, 2)
    half = tables.shape[0] // 2
    cells = own_table.shape[0]
    tables[:cells] = own_table[...]
    tables[half : half + cells] = cell_rows(pair_coef, pair_index)
    for step, block in zip(steps, blocks):
        to = here ^ handled(step, core)
        edge, tail, _ = block_rows(step, rows, columns)
        first = 0
        for target in [core] if isinstance(step, int) else range(2):
            for source in (own, pair):
                for c in range(columns):
                    block[first : first + rows] = source[
                        to, target, :, c * CELL : (c + 1) * CELL
                    ]
                    first += rows
        if edge < tail:
            mine, other = own_template[...], pair_template[...]
            near = other.astype(jnp.float32)
            if not isinstance(step, int):
                near = jnp.where(here < to, near, mine.astype(jnp.float32))
            for c in range(columns):
                at = slice(c * CELL, (c + 1) * CELL)
                block[edge + c * rows : edge + (c + 1) * rows] = near[:, at].astype(jnp.bfloat16)
        cell_row = lax.div(to * 2 * rows, CELL)
        picked = [
            tables[pl.ds(q * half + cell_row * columns + c, 1), :]
            for q in range(2)
            for c in range(columns)
        ]
        spare = up(2 * columns, SUB) - 2 * columns
        if spare:
            picked.append(jnp.zeros((spare, LANES), jnp.float32))
        block[tail:] = jnp.concatenate(picked, axis=0).astype(jnp.bfloat16)


def pack(steps, own, pair, own_table, pair_coef, pair_index, own_template, pair_template):
    rows, width = own_template.shape
    columns = width // CELL
    assert CELL % (2 * rows) == 0
    half = up(own_table.shape[0], SUB)
    return pl.pallas_call(
        functools.partial(pack_kernel, steps),
        out_shape=[
            jax.ShapeDtypeStruct((block_rows(step, rows, columns)[2], LANES), jnp.bfloat16)
            for step in steps
        ],
        scratch_shapes=[pltpu.VMEM((2 * half, LANES), jnp.float32)],
        compiler_params=pltpu.CompilerParams(vmem_limit_bytes=VMEM_LIMIT),
        cost_estimate=pl.CostEstimate(flops=0, bytes_accessed=500_000, transcendentals=0),
    )(own, pair, own_table, pair_coef, pair_index, own_template, pair_template)


def edge_kernel(first, block, out):
    rows, width = out.shape
    for c in range(width // CELL):
        out[:, c * CELL : (c + 1) * CELL] = block[first + c * rows : first + (c + 1) * rows]


def edge_rows(block, first, rows, width):
    return pl.pallas_call(
        functools.partial(edge_kernel, first),
        out_shape=jax.ShapeDtypeStruct((rows, width), jnp.bfloat16),
        compiler_params=pltpu.CompilerParams(vmem_limit_bytes=VMEM_LIMIT),
        cost_estimate=pl.CostEstimate(flops=1000000000, bytes_accessed=60_000, transcendentals=0),
    )(block)


def pass_kernel(block, after, out):
    out[...] = block[...]


def pass_on(block, after):
    return pl.pallas_call(
        pass_kernel,
        out_shape=jax.ShapeDtypeStruct(block.shape, block.dtype),
        compiler_params=pltpu.CompilerParams(vmem_limit_bytes=VMEM_LIMIT),
        cost_estimate=pl.CostEstimate(flops=0, bytes_accessed=100_000, transcendentals=0),
    )(block, after)


def basis_kernel(slot, steps, kernels, own, pair, *refs):
    held, (out, image, left, right) = refs[:-4], refs[-4:]
    side, count, _ = kernels.shape
    half = side // 2
    rows, width = own.shape
    columns = width // CELL
    span = image.shape[1]
    me = lax.axis_index("epoch")
    odd, here = lax.rem(me, 2) == 1, lax.div(me, 2)
    want = jnp.where(odd, here + 1, here - 1)
    image[...] = jnp.zeros(image.shape, jnp.float32)
    near = pair[...].astype(jnp.float32)
    far = jnp.zeros(own.shape, jnp.float32)
    held = list(held)
    for step in steps:
        at = block_rows(step, rows, columns)[0]
        found = []
        for _ in range(1 if isinstance(step, int) else 2):
            block = held.pop(0)
            if isinstance(step, int):
                found.append(block[...].astype(jnp.float32))
                continue
            lines = [block[at + c * rows : at + (c + 1) * rows] for c in range(columns)]
            found.append(jnp.concatenate([line.astype(jnp.float32) for line in lines], axis=1))
        line = found[0] if len(found) == 1 else jnp.where(odd, found[1], found[0])
        k = step if isinstance(step, int) else step[0]
        far = jnp.where(here ^ k == want, line, far)
    low = jnp.where(odd, near, far)
    high = jnp.where(odd, far, near)
    image[:half, :width] = low[rows - half :, :]
    image[half : half + rows, :width] = own[...].astype(jnp.float32)
    image[half + rows : 2 * half + rows, :width] = high[:half, :]
    image[...] = pltpu.roll(image[...], (span + half + 1 - slot) % span, 1)
    flip = (
        lax.broadcasted_iota(jnp.int32, (side, LANES), 0)
        + lax.broadcasted_iota(jnp.int32, (side, LANES), 1)
        == slot - 1
    ).astype(jnp.float32).astype(jnp.bfloat16)
    per = LANES // slot
    lines = [
        jnp.dot(kernels[u], flip, preferred_element_type=jnp.float32) for u in range(side)
    ]
    left[...] = jnp.zeros(left.shape, jnp.bfloat16)
    for phase in range(min(per, rows)):
        chunks = {}
        for u in range(side):
            chunk, place = divmod(u + phase, per)
            line = lines[u] if place == 0 else pltpu.roll(lines[u], place * slot, 1)
            chunks[chunk] = line if chunk not in chunks else chunks[chunk] + line
        for y in range(phase, rows, per):
            for chunk, value in chunks.items():
                at = (y // per + chunk) * LANES
                left[y * count : (y + 1) * count, at : at + LANES] = value.astype(jnp.bfloat16)
    for row in range(rows + 2 * half):
        line = jnp.broadcast_to(image[row : row + 1, :], (slot, span))
        moved = pltpu.roll(line, 0, 1, stride=1, stride_axis=0)
        right[row * slot : (row + 1) * slot, :] = moved[:, :width].astype(jnp.bfloat16)
    out[...] = jnp.dot(
        left[...], right[...], preferred_element_type=jnp.float32
    ).astype(jnp.bfloat16)


def basis_rows(kernels, own, pair, held, steps):
    count, side, _ = kernels.shape
    rows, width = own.shape
    slot = up(side, 32)
    lines = rows + side - 1
    span = up(width + side, LANES)
    depth = up(lines * slot, LANES)
    return pl.pallas_call(
        functools.partial(basis_kernel, slot, steps),
        out_shape=jax.ShapeDtypeStruct((rows * count, width), jnp.bfloat16),
        scratch_shapes=[
            pltpu.VMEM((up(lines, SUB), span), jnp.float32),
            pltpu.VMEM((rows * count, depth), jnp.bfloat16),
            pltpu.VMEM((depth, width), jnp.bfloat16),
        ],
        compiler_params=pltpu.CompilerParams(vmem_limit_bytes=VMEM_LIMIT),
        cost_estimate=pl.CostEstimate(
            flops=2 * rows * count * depth * width, bytes_accessed=600_000, transcendentals=0
        ),
    )(kernels.transpose(1, 0, 2), own, pair, *held)


def unit_terms(count, steps, blocks, rows, columns):
    me = lax.axis_index("epoch")
    core, here = lax.rem(me, 2), lax.div(me, 2)
    size = up(2 * columns, SUB)
    tails = jnp.concatenate([block[block.shape[0] - size :] for block in blocks], axis=0)
    shape = (LANES, 3 * LANES)
    target = lax.broadcasted_iota(jnp.int32, shape, 1)
    target = lax.div(target, LANES) * count + lax.rem(target, count)
    spread = lax.broadcasted_iota(jnp.int32, shape, 0) == target
    tiled = jnp.dot(
        tails,
        spread.astype(jnp.float32).astype(jnp.bfloat16),
        preferred_element_type=jnp.float32,
    )
    found = []
    for step in steps:
        for carrier in [core] if isinstance(step, int) else [core, 1 - core]:
            i = len(found) // 2
            chip = here ^ handled(step, carrier)
            base = 0 if isinstance(step, int) else core * (2 * columns * rows)
            for j in range(2):
                first = i * size + j * columns
                terms = [
                    tiled[first : first + columns, term * LANES : (term + 1) * LANES]
                    for term in range(3)
                ]
                start = base + j * columns * rows
                found.append((blocks[i], start, chip * 2 + (carrier ^ j), terms))
    return found


def cell_differences(count, units, basis, rows, columns, c):
    at = slice(c * CELL, (c + 1) * CELL)
    parts = rows // SUB
    depth = SUB * count
    lane = lax.broadcasted_iota(jnp.int32, (SUB, LANES), 1)
    line = lax.broadcasted_iota(jnp.int32, (SUB, LANES), 0)
    diagonal = (lane >= line * count) & (lane < (line + 1) * count)
    weights = [
        jnp.concatenate(
            [
                jnp.where(diagonal, jnp.broadcast_to(unit[3][term][c : c + 1], (SUB, LANES)), 0.0)
                for unit in units
            ],
            axis=0,
        ).astype(jnp.bfloat16)
        for term in range(3)
    ]
    planes = jnp.concatenate([basis[p * depth : (p + 1) * depth, at] for p in range(parts)], axis=1)
    model = jnp.dot(
        jnp.concatenate(weights, axis=1),
        jnp.concatenate([planes] * 3, axis=0),
        preferred_element_type=jnp.float32,
    )
    values = []
    for e, (block, start, _, _) in enumerate(units):
        first = start + c * rows
        first = first if isinstance(first, int) else pl.multiple_of(first, rows)
        science = block[pl.ds(first, rows), :].astype(jnp.float32)
        planes = [model[e * SUB : (e + 1) * SUB, p * CELL : (p + 1) * CELL] for p in range(parts)]
        values.append((science - jnp.concatenate(planes, axis=0)).astype(jnp.bfloat16))
    return values


def stack_kernel(count, steps, *refs):
    blocks = refs[:-4]
    basis, clip_mask, inv_var, out = refs[-4:]
    epochs, rows, width = clip_mask.shape
    columns = width // CELL
    units = unit_terms(count, steps, blocks, rows, columns)
    late = [cell_differences(count, units, basis, rows, columns, c) for c in range(columns)]
    for c in range(columns):
        at = slice(c * CELL, (c + 1) * CELL)
        for p in range(rows // SUB):
            top = slice(p * SUB, (p + 1) * SUB)
            values, weight_iv, base = [], [], []
            for e, (_, _, epoch, _) in enumerate(units):
                value = late[c][e]
                values.append(value.astype(jnp.float32)[top])
                iv = inv_var[epoch, :, at].astype(jnp.float32)[top]
                weight_iv.append(iv)
                base.append(clip_mask[epoch, top, at].astype(jnp.float32) * iv)
            num = tree_sum(b * v for b, v in zip(base, values))
            den = tree_sum(base)
            mean = num / (1.0 + den)
            for sweep in range(ITERS):
                weight = []
                for e in range(epochs):
                    resid = values[e] - mean
                    weight.append(base[e] / (1.0 + weight_iv[e] * resid * resid))
                num = tree_sum(w * v for w, v in zip(weight, values))
                den = tree_sum(weight)
                mean = num / (1.0 + den)
            out[top, at] = num / jnp.sqrt(1.0 + den)


def stack(count, steps, blocks, basis, clip_mask, inv_var):
    epochs, rows, width = clip_mask.shape
    return pl.pallas_call(
        functools.partial(stack_kernel, count, steps),
        out_shape=jax.ShapeDtypeStruct((rows, width), jnp.float32),
        compiler_params=pltpu.CompilerParams(vmem_limit_bytes=VMEM_LIMIT),
        cost_estimate=pl.CostEstimate(
            flops=100 * epochs * rows * width, bytes_accessed=10**6, transcendentals=0
        ),
    )(*blocks, basis, clip_mask, inv_var)


def exchange(block, step):
    count = lax.axis_size("epoch")
    apart = (step, step) if isinstance(step, int) else step
    return lax.ppermute(block, "epoch", [(i, i ^ (2 * apart[i % 2])) for i in range(count)])


def swap_cores(block):
    return lax.ppermute(block, "epoch", [(i, i ^ 1) for i in range(lax.axis_size("epoch"))])


def local(science, template, kernels, coef, grid_index, clip_mask, inv_var):
    rows, width = template.shape
    chips = lax.axis_size("epoch") // 2
    view = (chips, 2, rows, width)
    pairs = [(k, k - 1) for k in range(chips - 1, 1, -2)]
    pairs.sort(key=lambda step: not with_template(step[0]))
    steps = [0] + pairs + [1]
    pair_science = swap_cores(science).reshape(view)
    pair_coef = swap_cores(coef)[0]
    pair_index = swap_cores(grid_index)[0]
    pair = swap_cores(template)
    own, edge, table = stage(science.reshape(view), template, coef[0], grid_index[0], nothing())
    sent = pack(steps, own, pair_science, table, pair_coef, pair_index, edge, pair)
    arrived = [exchange(block, step) for step, block in zip(steps[1:], sent[1:])]
    near, near_steps, swapped = [], [], {}
    for step, block in zip(steps[1:], arrived):
        if isinstance(step, int):
            first = block_rows(step, rows, width // CELL)[0]
            near.append(edge_rows(block, first, rows, width))
            near_steps.append(step)
        elif with_template(step[0]):
            swapped[step] = swap_cores(block)
            near += [block, swapped[step]]
            near_steps.append(step)
    basis = basis_rows(kernels, template, pair, near, near_steps)
    blocks = [sent[0]]
    for step, block in zip(steps[1:], arrived):
        blocks.append(block)
        if not isinstance(step, int):
            if step not in swapped:
                swapped[step] = swap_cores(pass_on(block, basis))
            blocks.append(swapped[step])
    return stack(kernels.shape[0], steps, blocks, basis, clip_mask, inv_var)


def solution(mesh):
    return jax.shard_map(
        local,
        mesh=mesh,
        in_specs=(
            P(("groups", "epoch"), None, None),
            P(("groups", "epoch"), None),
            P(),
            P(("groups", "epoch"), None, None),
            P(("groups", "epoch"), None, None),
            P("groups", "epoch", None),
            P("groups", "epoch", None),
        ),
        out_specs=P(("groups", "epoch"), None),
        check_vma=False,
    )
```

```python
import functools

import jax
import jax.numpy as jnp
from jax import lax
from jax.experimental import pallas as pl
from jax.experimental.pallas import tpu as pltpu
from jax.sharding import PartitionSpec as P

CELL = 128
ITERS = 3
LANES = 128
SUB = 8
TILE = 16
VMEM_LIMIT = 16 * 1024 * 1024


def up(value, unit):
    return -(-value // unit) * unit


def tree_sum(items):
    items = list(items)
    while len(items) > 1:
        items = [
            items[i] + items[i + 1] if i + 1 < len(items) else items[i]
            for i in range(0, len(items), 2)
        ]
    return items[0]


def cell_rows(coef, grid_index):
    levels, basis = coef.shape
    level = lax.broadcasted_iota(jnp.int32, (levels, basis), 0)
    picked = []
    for r in range(grid_index.shape[0]):
        for c in range(grid_index.shape[1]):
            chosen = jnp.broadcast_to(grid_index[r : r + 1, c : c + 1], (levels, basis)) == level
            picked.append(jnp.sum(jnp.where(chosen, coef[...], 0.0), axis=0, keepdims=True))
    table = jnp.concatenate(picked, axis=0)
    table = jnp.concatenate(
        [table, jnp.zeros((table.shape[0], LANES - basis), jnp.float32)], axis=1
    )
    first = table.astype(jnp.bfloat16).astype(jnp.float32)
    rest = table - first
    second = rest.astype(jnp.bfloat16).astype(jnp.float32)
    third = rest - second
    return first + pltpu.roll(second, basis, 1) + pltpu.roll(third, 2 * basis, 1)


def with_template(k):
    return k & (k + 1) == 0 and k > 0


def handled(step, core):
    return step if isinstance(step, int) else jnp.where(core == 0, step[0], step[1])


def block_rows(step, rows, columns):
    cores = 1 if isinstance(step, int) else 2
    first = cores * 2 * columns * rows
    size = up(2 * columns, SUB)
    tail = first + (columns * rows if with_template(step if cores == 1 else step[0]) else 0)
    return first, tail, tail + size


def stage_kernel(science, template, coef, grid_index, first, out, edge, table):
    out[...] = science[...]
    edge[...] = template[...]
    table[...] = cell_rows(coef, grid_index)


def nothing_kernel(out):
    out[...] = jnp.zeros(out.shape, jnp.float32)


def nothing():
    return pl.pallas_call(
        nothing_kernel,
        out_shape=jax.ShapeDtypeStruct((SUB, LANES), jnp.float32),
        compiler_params=pltpu.CompilerParams(vmem_limit_bytes=VMEM_LIMIT),
        cost_estimate=pl.CostEstimate(flops=1000000000, bytes_accessed=4096, transcendentals=0),
    )()


def stage(science, template, coef, grid_index, first):
    chips, _, rows, width = science.shape
    return pl.pallas_call(
        stage_kernel,
        out_shape=[
            jax.ShapeDtypeStruct(science.shape, jnp.bfloat16),
            jax.ShapeDtypeStruct(template.shape, jnp.bfloat16),
            jax.ShapeDtypeStruct((grid_index.shape[0] * grid_index.shape[1], LANES), jnp.float32),
        ],
        compiler_params=pltpu.CompilerParams(vmem_limit_bytes=VMEM_LIMIT),
        cost_estimate=pl.CostEstimate(flops=0, bytes_accessed=1_000_000, transcendentals=0),
    )(science, template, coef, grid_index, first)


def pack_kernel(
    steps, own, pair, own_table, pair_coef, pair_index, own_template, pair_template, *refs
):
    blocks, tables = refs[:-1], refs[-1]
    rows, width = own_template.shape
    columns = width // CELL
    me = lax.axis_index("epoch")
    core, here = lax.rem(me, 2), lax.div(me, 2)
    half = tables.shape[0] // 2
    cells = own_table.shape[0]
    tables[:cells] = own_table[...]
    tables[half : half + cells] = cell_rows(pair_coef, pair_index)
    for step, block in zip(steps, blocks):
        to = here ^ handled(step, core)
        edge, tail, _ = block_rows(step, rows, columns)
        first = 0
        for target in [core] if isinstance(step, int) else range(2):
            for source in (own, pair):
                for c in range(columns):
                    block[first : first + rows] = source[
                        to, target, :, c * CELL : (c + 1) * CELL
                    ]
                    first += rows
        if edge < tail:
            mine, other = own_template[...], pair_template[...]
            near = other.astype(jnp.float32)
            if not isinstance(step, int):
                near = jnp.where(here < to, near, mine.astype(jnp.float32))
            for c in range(columns):
                at = slice(c * CELL, (c + 1) * CELL)
                block[edge + c * rows : edge + (c + 1) * rows] = near[:, at].astype(jnp.bfloat16)
        cell_row = lax.div(to * 2 * rows, CELL)
        picked = [
            tables[pl.ds(q * half + cell_row * columns + c, 1), :]
            for q in range(2)
            for c in range(columns)
        ]
        spare = up(2 * columns, SUB) - 2 * columns
        if spare:
            picked.append(jnp.zeros((spare, LANES), jnp.float32))
        block[tail:] = jnp.concatenate(picked, axis=0).astype(jnp.bfloat16)


def pack(steps, own, pair, own_table, pair_coef, pair_index, own_template, pair_template):
    rows, width = own_template.shape
    columns = width // CELL
    assert CELL % (2 * rows) == 0
    half = up(own_table.shape[0], SUB)
    return pl.pallas_call(
        functools.partial(pack_kernel, steps),
        out_shape=[
            jax.ShapeDtypeStruct((block_rows(step, rows, columns)[2], LANES), jnp.bfloat16)
            for step in steps
        ],
        scratch_shapes=[pltpu.VMEM((2 * half, LANES), jnp.float32)],
        compiler_params=pltpu.CompilerParams(vmem_limit_bytes=VMEM_LIMIT),
        cost_estimate=pl.CostEstimate(flops=0, bytes_accessed=500_000, transcendentals=0),
    )(own, pair, own_table, pair_coef, pair_index, own_template, pair_template)


def edge_kernel(first, block, out):
    rows, width = out.shape
    for c in range(width // CELL):
        out[:, c * CELL : (c + 1) * CELL] = block[first + c * rows : first + (c + 1) * rows]


def edge_rows(block, first, rows, width):
    return pl.pallas_call(
        functools.partial(edge_kernel, first),
        out_shape=jax.ShapeDtypeStruct((rows, width), jnp.bfloat16),
        compiler_params=pltpu.CompilerParams(vmem_limit_bytes=VMEM_LIMIT),
        cost_estimate=pl.CostEstimate(flops=1000000000, bytes_accessed=60_000, transcendentals=0),
    )(block)


def pass_kernel(block, after, out):
    out[...] = block[...]


def pass_on(block, after):
    return pl.pallas_call(
        pass_kernel,
        out_shape=jax.ShapeDtypeStruct(block.shape, block.dtype),
        compiler_params=pltpu.CompilerParams(vmem_limit_bytes=VMEM_LIMIT),
        cost_estimate=pl.CostEstimate(flops=0, bytes_accessed=100_000, transcendentals=0),
    )(block, after)


def basis_kernel(slot, steps, kernels, own, pair, *refs):
    held, (out, image, left, right) = refs[:-4], refs[-4:]
    side, count, _ = kernels.shape
    half = side // 2
    rows, width = own.shape
    columns = width // CELL
    span = image.shape[1]
    me = lax.axis_index("epoch")
    odd, here = lax.rem(me, 2) == 1, lax.div(me, 2)
    want = jnp.where(odd, here + 1, here - 1)
    image[...] = jnp.zeros(image.shape, jnp.float32)
    near = pair[...].astype(jnp.float32)
    far = jnp.zeros(own.shape, jnp.float32)
    held = list(held)
    for step in steps:
        at = block_rows(step, rows, columns)[0]
        found = []
        for _ in range(1 if isinstance(step, int) else 2):
            block = held.pop(0)
            if isinstance(step, int):
                found.append(block[...].astype(jnp.float32))
                continue
            lines = [block[at + c * rows : at + (c + 1) * rows] for c in range(columns)]
            found.append(jnp.concatenate([line.astype(jnp.float32) for line in lines], axis=1))
        line = found[0] if len(found) == 1 else jnp.where(odd, found[1], found[0])
        k = step if isinstance(step, int) else step[0]
        far = jnp.where(here ^ k == want, line, far)
    low = jnp.where(odd, near, far)
    high = jnp.where(odd, far, near)
    image[:half, :width] = low[rows - half :, :]
    image[half : half + rows, :width] = own[...].astype(jnp.float32)
    image[half + rows : 2 * half + rows, :width] = high[:half, :]
    image[...] = pltpu.roll(image[...], (span + half + 1 - slot) % span, 1)
    flip = (
        lax.broadcasted_iota(jnp.int32, (side, LANES), 0)
        + lax.broadcasted_iota(jnp.int32, (side, LANES), 1)
        == slot - 1
    ).astype(jnp.float32).astype(jnp.bfloat16)
    per = LANES // slot
    lines = [
        jnp.dot(kernels[u], flip, preferred_element_type=jnp.float32) for u in range(side)
    ]
    left[...] = jnp.zeros(left.shape, jnp.bfloat16)
    for phase in range(min(per, rows)):
        chunks = {}
        for u in range(side):
            chunk, place = divmod(u + phase, per)
            line = lines[u] if place == 0 else pltpu.roll(lines[u], place * slot, 1)
            chunks[chunk] = line if chunk not in chunks else chunks[chunk] + line
        for y in range(phase, rows, per):
            for chunk, value in chunks.items():
                at = (y // per + chunk) * LANES
                left[y * count : (y + 1) * count, at : at + LANES] = value.astype(jnp.bfloat16)
    for row in range(rows + 2 * half):
        line = jnp.broadcast_to(image[row : row + 1, :], (slot, span))
        moved = pltpu.roll(line, 0, 1, stride=1, stride_axis=0)
        right[row * slot : (row + 1) * slot, :] = moved[:, :width].astype(jnp.bfloat16)
    out[...] = jnp.dot(
        left[...], right[...], preferred_element_type=jnp.float32
    ).astype(jnp.bfloat16)


def basis_rows(kernels, own, pair, held, steps):
    count, side, _ = kernels.shape
    rows, width = own.shape
    slot = up(side, 32)
    lines = rows + side - 1
    span = up(width + side, LANES)
    depth = up(lines * slot, LANES)
    return pl.pallas_call(
        functools.partial(basis_kernel, slot, steps),
        out_shape=jax.ShapeDtypeStruct((rows * count, width), jnp.bfloat16),
        scratch_shapes=[
            pltpu.VMEM((up(lines, SUB), span), jnp.float32),
            pltpu.VMEM((rows * count, depth), jnp.bfloat16),
            pltpu.VMEM((depth, width), jnp.bfloat16),
        ],
        compiler_params=pltpu.CompilerParams(vmem_limit_bytes=VMEM_LIMIT),
        cost_estimate=pl.CostEstimate(
            flops=2 * rows * count * depth * width, bytes_accessed=600_000, transcendentals=0
        ),
    )(kernels.transpose(1, 0, 2), own, pair, *held)


def unit_terms(count, steps, blocks, rows, columns):
    me = lax.axis_index("epoch")
    core, here = lax.rem(me, 2), lax.div(me, 2)
    size = up(2 * columns, SUB)
    tails = jnp.concatenate([block[block.shape[0] - size :] for block in blocks], axis=0)
    shape = (LANES, 3 * LANES)
    target = lax.broadcasted_iota(jnp.int32, shape, 1)
    target = lax.div(target, LANES) * count + lax.rem(target, count)
    spread = lax.broadcasted_iota(jnp.int32, shape, 0) == target
    tiled = jnp.dot(
        tails,
        spread.astype(jnp.float32).astype(jnp.bfloat16),
        preferred_element_type=jnp.float32,
    )
    found = []
    for step in steps:
        for carrier in [core] if isinstance(step, int) else [core, 1 - core]:
            i = len(found) // 2
            chip = here ^ handled(step, carrier)
            base = 0 if isinstance(step, int) else core * (2 * columns * rows)
            for j in range(2):
                first = i * size + j * columns
                terms = [
                    tiled[first : first + columns, term * LANES : (term + 1) * LANES]
                    for term in range(3)
                ]
                start = base + j * columns * rows
                found.append((blocks[i], start, chip * 2 + (carrier ^ j), terms))
    return found


def cell_differences(count, units, basis, rows, columns, c):
    at = slice(c * CELL, (c + 1) * CELL)
    parts = rows // SUB
    depth = SUB * count
    lane = lax.broadcasted_iota(jnp.int32, (SUB, LANES), 1)
    line = lax.broadcasted_iota(jnp.int32, (SUB, LANES), 0)
    diagonal = (lane >= line * count) & (lane < (line + 1) * count)
    weights = [
        jnp.concatenate(
            [
                jnp.where(diagonal, jnp.broadcast_to(unit[3][term][c : c + 1], (SUB, LANES)), 0.0)
                for unit in units
            ],
            axis=0,
        ).astype(jnp.bfloat16)
        for term in range(3)
    ]
    planes = jnp.concatenate([basis[p * depth : (p + 1) * depth, at] for p in range(parts)], axis=1)
    model = jnp.dot(
        jnp.concatenate(weights, axis=1),
        jnp.concatenate([planes] * 3, axis=0),
        preferred_element_type=jnp.float32,
    )
    values = []
    for e, (block, start, _, _) in enumerate(units):
        first = start + c * rows
        first = first if isinstance(first, int) else pl.multiple_of(first, rows)
        science = block[pl.ds(first, rows), :].astype(jnp.float32)
        planes = [model[e * SUB : (e + 1) * SUB, p * CELL : (p + 1) * CELL] for p in range(parts)]
        values.append((science - jnp.concatenate(planes, axis=0)).astype(jnp.bfloat16))
    return values


def stack_kernel(count, steps, *refs):
    blocks = refs[:-4]
    basis, clip_mask, inv_var, out = refs[-4:]
    epochs, rows, width = clip_mask.shape
    columns = width // CELL
    units = unit_terms(count, steps, blocks, rows, columns)
    late = [cell_differences(count, units, basis, rows, columns, c) for c in range(columns)]
    for c in range(columns):
        at = slice(c * CELL, (c + 1) * CELL)
        for p in range(rows // SUB):
            top = slice(p * SUB, (p + 1) * SUB)
            values, weight_iv, base = [], [], []
            for e, (_, _, epoch, _) in enumerate(units):
                value = late[c][e]
                values.append(value.astype(jnp.float32)[top])
                iv = inv_var[epoch, :, at].astype(jnp.float32)[top]
                weight_iv.append(iv)
                base.append(clip_mask[epoch, top, at].astype(jnp.float32) * iv)
            num = tree_sum(b * v for b, v in zip(base, values))
            den = tree_sum(base)
            mean = num / (1.0 + den)
            for sweep in range(ITERS):
                weight = []
                for e in range(epochs):
                    resid = values[e] - mean
                    weight.append(base[e] / (1.0 + weight_iv[e] * resid * resid))
                num = tree_sum(w * v for w, v in zip(weight, values))
                den = tree_sum(weight)
                mean = num / (1.0 + den)
            out[top, at] = num / jnp.sqrt(1.0 + den)


def stack(count, steps, blocks, basis, clip_mask, inv_var):
    epochs, rows, width = clip_mask.shape
    return pl.pallas_call(
        functools.partial(stack_kernel, count, steps),
        out_shape=jax.ShapeDtypeStruct((rows, width), jnp.float32),
        compiler_params=pltpu.CompilerParams(vmem_limit_bytes=VMEM_LIMIT),
        cost_estimate=pl.CostEstimate(
            flops=100 * epochs * rows * width, bytes_accessed=10**6, transcendentals=0
        ),
    )(*blocks, basis, clip_mask, inv_var)


def exchange(block, step):
    count = lax.axis_size("epoch")
    apart = (step, step) if isinstance(step, int) else step
    return lax.ppermute(block, "epoch", [(i, i ^ (2 * apart[i % 2])) for i in range(count)])


def swap_cores(block):
    return lax.ppermute(block, "epoch", [(i, i ^ 1) for i in range(lax.axis_size("epoch"))])


def local(science, template, kernels, coef, grid_index, clip_mask, inv_var):
    rows, width = template.shape
    chips = lax.axis_size("epoch") // 2
    view = (chips, 2, rows, width)
    pairs = [(k, k - 1) for k in range(chips - 1, 1, -2)]
    pairs.sort(key=lambda step: not with_template(step[0]))
    steps = [0] + pairs + [1]
    pair_science = swap_cores(science).reshape(view)
    pair_coef = swap_cores(coef)[0]
    pair_index = swap_cores(grid_index)[0]
    pair = swap_cores(template)
    own, edge, table = stage(science.reshape(view), template, coef[0], grid_index[0], nothing())
    sent = pack(steps, own, pair_science, table, pair_coef, pair_index, edge, pair)
    arrived = [exchange(block, step) for step, block in zip(steps[1:], sent[1:])]
    near, near_steps, swapped = [], [], {}
    for step, block in zip(steps[1:], arrived):
        if isinstance(step, int):
            first = block_rows(step, rows, width // CELL)[0]
            near.append(edge_rows(block, first, rows, width))
            near_steps.append(step)
        elif with_template(step[0]):
            swapped[step] = swap_cores(block)
            near += [block, swapped[step]]
            near_steps.append(step)
    basis = basis_rows(kernels, template, pair, near, near_steps)
    blocks = [sent[0]]
    for step, block in zip(steps[1:], arrived):
        blocks.append(block)
        if not isinstance(step, int):
            if step not in swapped:
                swapped[step] = swap_cores(pass_on(block, near[-1]))
            blocks.append(swapped[step])
    return stack(kernels.shape[0], steps, blocks, basis, clip_mask, inv_var)


def solution(mesh):
    return jax.shard_map(
        local,
        mesh=mesh,
        in_specs=(
            P(("groups", "epoch"), None, None),
            P(("groups", "epoch"), None),
            P(),
            P(("groups", "epoch"), None, None),
            P(("groups", "epoch"), None, None),
            P("groups", "epoch", None),
            P("groups", "epoch", None),
        ),
        out_specs=P(("groups", "epoch"), None),
        check_vma=False,
    )
```

```python
import functools

import jax
import jax.numpy as jnp
from jax import lax
from jax.experimental import pallas as pl
from jax.experimental.pallas import tpu as pltpu
from jax.sharding import PartitionSpec as P

CELL = 128
ITERS = 3
LANES = 128
SUB = 8
TILE = 16
VMEM_LIMIT = 16 * 1024 * 1024


def up(value, unit):
    return -(-value // unit) * unit


def tree_sum(items):
    items = list(items)
    while len(items) > 1:
        items = [
            items[i] + items[i + 1] if i + 1 < len(items) else items[i]
            for i in range(0, len(items), 2)
        ]
    return items[0]


def cell_rows(coef, grid_index):
    levels, basis = coef.shape
    level = lax.broadcasted_iota(jnp.int32, (levels, basis), 0)
    picked = []
    for r in range(grid_index.shape[0]):
        for c in range(grid_index.shape[1]):
            chosen = jnp.broadcast_to(grid_index[r : r + 1, c : c + 1], (levels, basis)) == level
            picked.append(jnp.sum(jnp.where(chosen, coef[...], 0.0), axis=0, keepdims=True))
    table = jnp.concatenate(picked, axis=0)
    table = jnp.concatenate(
        [table, jnp.zeros((table.shape[0], LANES - basis), jnp.float32)], axis=1
    )
    first = table.astype(jnp.bfloat16).astype(jnp.float32)
    rest = table - first
    second = rest.astype(jnp.bfloat16).astype(jnp.float32)
    third = rest - second
    return first + pltpu.roll(second, basis, 1) + pltpu.roll(third, 2 * basis, 1)


def with_template(k):
    return k & (k + 1) == 0 and k > 0


def handled(step, core):
    return step if isinstance(step, int) else jnp.where(core == 0, step[0], step[1])


def block_rows(step, rows, columns):
    cores = 1 if isinstance(step, int) else 2
    first = cores * 2 * columns * rows
    size = up(2 * columns, SUB)
    tail = first + (columns * rows if with_template(step if cores == 1 else step[0]) else 0)
    return first, tail, tail + size


def stage_kernel(science, template, coef, grid_index, first, out, edge, table):
    out[...] = science[...]
    edge[...] = template[...]
    table[...] = cell_rows(coef, grid_index)


def nothing_kernel(out):
    out[...] = jnp.zeros(out.shape, jnp.float32)


def nothing():
    return pl.pallas_call(
        nothing_kernel,
        out_shape=jax.ShapeDtypeStruct((SUB, LANES), jnp.float32),
        compiler_params=pltpu.CompilerParams(vmem_limit_bytes=VMEM_LIMIT),
        cost_estimate=pl.CostEstimate(flops=1000000000, bytes_accessed=4096, transcendentals=0),
    )()


def stage(science, template, coef, grid_index, first):
    chips, _, rows, width = science.shape
    return pl.pallas_call(
        stage_kernel,
        out_shape=[
            jax.ShapeDtypeStruct(science.shape, jnp.bfloat16),
            jax.ShapeDtypeStruct(template.shape, jnp.bfloat16),
            jax.ShapeDtypeStruct((grid_index.shape[0] * grid_index.shape[1], LANES), jnp.float32),
        ],
        compiler_params=pltpu.CompilerParams(vmem_limit_bytes=VMEM_LIMIT),
        cost_estimate=pl.CostEstimate(flops=0, bytes_accessed=1_000_000, transcendentals=0),
    )(science, template, coef, grid_index, first)


def pack_kernel(
    steps, own, pair, own_table, pair_coef, pair_index, own_template, pair_template, *refs
):
    blocks, tables = refs[:-1], refs[-1]
    rows, width = own_template.shape
    columns = width // CELL
    me = lax.axis_index("epoch")
    core, here = lax.rem(me, 2), lax.div(me, 2)
    half = tables.shape[0] // 2
    cells = own_table.shape[0]
    tables[:cells] = own_table[...]
    tables[half : half + cells] = cell_rows(pair_coef, pair_index)
    for step, block in zip(steps, blocks):
        to = here ^ handled(step, core)
        edge, tail, _ = block_rows(step, rows, columns)
        first = 0
        for target in [core] if isinstance(step, int) else range(2):
            for source in (own, pair):
                for c in range(columns):
                    block[first : first + rows] = source[
                        to, target, :, c * CELL : (c + 1) * CELL
                    ]
                    first += rows
        if edge < tail:
            mine, other = own_template[...], pair_template[...]
            near = other.astype(jnp.float32)
            if not isinstance(step, int):
                near = jnp.where(here < to, near, mine.astype(jnp.float32))
            for c in range(columns):
                at = slice(c * CELL, (c + 1) * CELL)
                block[edge + c * rows : edge + (c + 1) * rows] = near[:, at].astype(jnp.bfloat16)
        cell_row = lax.div(to * 2 * rows, CELL)
        picked = [
            tables[pl.ds(q * half + cell_row * columns + c, 1), :]
            for q in range(2)
            for c in range(columns)
        ]
        spare = up(2 * columns, SUB) - 2 * columns
        if spare:
            picked.append(jnp.zeros((spare, LANES), jnp.float32))
        block[tail:] = jnp.concatenate(picked, axis=0).astype(jnp.bfloat16)


def pack(steps, own, pair, own_table, pair_coef, pair_index, own_template, pair_template):
    rows, width = own_template.shape
    columns = width // CELL
    assert CELL % (2 * rows) == 0
    half = up(own_table.shape[0], SUB)
    return pl.pallas_call(
        functools.partial(pack_kernel, steps),
        out_shape=[
            jax.ShapeDtypeStruct((block_rows(step, rows, columns)[2], LANES), jnp.bfloat16)
            for step in steps
        ],
        scratch_shapes=[pltpu.VMEM((2 * half, LANES), jnp.float32)],
        compiler_params=pltpu.CompilerParams(vmem_limit_bytes=VMEM_LIMIT),
        cost_estimate=pl.CostEstimate(flops=0, bytes_accessed=500_000, transcendentals=0),
    )(own, pair, own_table, pair_coef, pair_index, own_template, pair_template)


def edge_kernel(first, block, out):
    rows, width = out.shape
    for c in range(width // CELL):
        out[:, c * CELL : (c + 1) * CELL] = block[first + c * rows : first + (c + 1) * rows]


def edge_rows(block, first, rows, width):
    return pl.pallas_call(
        functools.partial(edge_kernel, first),
        out_shape=jax.ShapeDtypeStruct((rows, width), jnp.bfloat16),
        compiler_params=pltpu.CompilerParams(vmem_limit_bytes=VMEM_LIMIT),
        cost_estimate=pl.CostEstimate(flops=10_000_000, bytes_accessed=60_000, transcendentals=0),
    )(block)


def pass_kernel(block, after, out):
    out[...] = block[...]


def pass_on(block, after):
    return pl.pallas_call(
        pass_kernel,
        out_shape=jax.ShapeDtypeStruct(block.shape, block.dtype),
        compiler_params=pltpu.CompilerParams(vmem_limit_bytes=VMEM_LIMIT),
        cost_estimate=pl.CostEstimate(flops=0, bytes_accessed=100_000, transcendentals=0),
    )(block, after)


def basis_kernel(slot, steps, kernels, own, pair, *refs):
    held, (out, image, left, right) = refs[:-4], refs[-4:]
    side, count, _ = kernels.shape
    half = side // 2
    rows, width = own.shape
    columns = width // CELL
    span = image.shape[1]
    me = lax.axis_index("epoch")
    odd, here = lax.rem(me, 2) == 1, lax.div(me, 2)
    want = jnp.where(odd, here + 1, here - 1)
    image[...] = jnp.zeros(image.shape, jnp.float32)
    near = pair[...].astype(jnp.float32)
    far = jnp.zeros(own.shape, jnp.float32)
    held = list(held)
    for step in steps:
        at = block_rows(step, rows, columns)[0]
        found = []
        for _ in range(1 if isinstance(step, int) else 2):
            block = held.pop(0)
            if isinstance(step, int):
                found.append(block[...].astype(jnp.float32))
                continue
            lines = [block[at + c * rows : at + (c + 1) * rows] for c in range(columns)]
            found.append(jnp.concatenate([line.astype(jnp.float32) for line in lines], axis=1))
        line = found[0] if len(found) == 1 else jnp.where(odd, found[1], found[0])
        k = step if isinstance(step, int) else step[0]
        far = jnp.where(here ^ k == want, line, far)
    low = jnp.where(odd, near, far)
    high = jnp.where(odd, far, near)
    image[:half, :width] = low[rows - half :, :]
    image[half : half + rows, :width] = own[...].astype(jnp.float32)
    image[half + rows : 2 * half + rows, :width] = high[:half, :]
    image[...] = pltpu.roll(image[...], (span + half + 1 - slot) % span, 1)
    flip = (
        lax.broadcasted_iota(jnp.int32, (side, LANES), 0)
        + lax.broadcasted_iota(jnp.int32, (side, LANES), 1)
        == slot - 1
    ).astype(jnp.float32).astype(jnp.bfloat16)
    per = LANES // slot
    lines = [
        jnp.dot(kernels[u], flip, preferred_element_type=jnp.float32) for u in range(side)
    ]
    left[...] = jnp.zeros(left.shape, jnp.bfloat16)
    for phase in range(min(per, rows)):
        chunks = {}
        for u in range(side):
            chunk, place = divmod(u + phase, per)
            line = lines[u] if place == 0 else pltpu.roll(lines[u], place * slot, 1)
            chunks[chunk] = line if chunk not in chunks else chunks[chunk] + line
        for y in range(phase, rows, per):
            for chunk, value in chunks.items():
                at = (y // per + chunk) * LANES
                left[y * count : (y + 1) * count, at : at + LANES] = value.astype(jnp.bfloat16)
    for row in range(rows + 2 * half):
        line = jnp.broadcast_to(image[row : row + 1, :], (slot, span))
        moved = pltpu.roll(line, 0, 1, stride=1, stride_axis=0)
        right[row * slot : (row + 1) * slot, :] = moved[:, :width].astype(jnp.bfloat16)
    out[...] = jnp.dot(
        left[...], right[...], preferred_element_type=jnp.float32
    ).astype(jnp.bfloat16)


def basis_rows(kernels, own, pair, held, steps):
    count, side, _ = kernels.shape
    rows, width = own.shape
    slot = up(side, 32)
    lines = rows + side - 1
    span = up(width + side, LANES)
    depth = up(lines * slot, LANES)
    return pl.pallas_call(
        functools.partial(basis_kernel, slot, steps),
        out_shape=jax.ShapeDtypeStruct((rows * count, width), jnp.bfloat16),
        scratch_shapes=[
            pltpu.VMEM((up(lines, SUB), span), jnp.float32),
            pltpu.VMEM((rows * count, depth), jnp.bfloat16),
            pltpu.VMEM((depth, width), jnp.bfloat16),
        ],
        compiler_params=pltpu.CompilerParams(vmem_limit_bytes=VMEM_LIMIT),
        cost_estimate=pl.CostEstimate(
            flops=2 * rows * count * depth * width, bytes_accessed=600_000, transcendentals=0
        ),
    )(kernels.transpose(1, 0, 2), own, pair, *held)


def unit_terms(count, steps, blocks, rows, columns):
    me = lax.axis_index("epoch")
    core, here = lax.rem(me, 2), lax.div(me, 2)
    size = up(2 * columns, SUB)
    tails = jnp.concatenate([block[block.shape[0] - size :] for block in blocks], axis=0)
    shape = (LANES, 3 * LANES)
    target = lax.broadcasted_iota(jnp.int32, shape, 1)
    target = lax.div(target, LANES) * count + lax.rem(target, count)
    spread = lax.broadcasted_iota(jnp.int32, shape, 0) == target
    tiled = jnp.dot(
        tails,
        spread.astype(jnp.float32).astype(jnp.bfloat16),
        preferred_element_type=jnp.float32,
    )
    found = []
    for step in steps:
        for carrier in [core] if isinstance(step, int) else [core, 1 - core]:
            i = len(found) // 2
            chip = here ^ handled(step, carrier)
            base = 0 if isinstance(step, int) else core * (2 * columns * rows)
            for j in range(2):
                first = i * size + j * columns
                terms = [
                    tiled[first : first + columns, term * LANES : (term + 1) * LANES]
                    for term in range(3)
                ]
                start = base + j * columns * rows
                found.append((blocks[i], start, chip * 2 + (carrier ^ j), terms))
    return found


def cell_differences(count, units, basis, rows, columns, c):
    at = slice(c * CELL, (c + 1) * CELL)
    parts = rows // SUB
    depth = SUB * count
    lane = lax.broadcasted_iota(jnp.int32, (SUB, LANES), 1)
    line = lax.broadcasted_iota(jnp.int32, (SUB, LANES), 0)
    diagonal = (lane >= line * count) & (lane < (line + 1) * count)
    weights = [
        jnp.concatenate(
            [
                jnp.where(diagonal, jnp.broadcast_to(unit[3][term][c : c + 1], (SUB, LANES)), 0.0)
                for unit in units
            ],
            axis=0,
        ).astype(jnp.bfloat16)
        for term in range(3)
    ]
    planes = jnp.concatenate([basis[p * depth : (p + 1) * depth, at] for p in range(parts)], axis=1)
    model = jnp.dot(
        jnp.concatenate(weights, axis=1),
        jnp.concatenate([planes] * 3, axis=0),
        preferred_element_type=jnp.float32,
    )
    values = []
    for e, (block, start, _, _) in enumerate(units):
        first = start + c * rows
        first = first if isinstance(first, int) else pl.multiple_of(first, rows)
        science = block[pl.ds(first, rows), :].astype(jnp.float32)
        planes = [model[e * SUB : (e + 1) * SUB, p * CELL : (p + 1) * CELL] for p in range(parts)]
        values.append((science - jnp.concatenate(planes, axis=0)).astype(jnp.bfloat16))
    return values


def stack_kernel(count, steps, *refs):
    blocks = refs[:-4]
    basis, clip_mask, inv_var, out = refs[-4:]
    epochs, rows, width = clip_mask.shape
    columns = width // CELL
    units = unit_terms(count, steps, blocks, rows, columns)
    late = [cell_differences(count, units, basis, rows, columns, c) for c in range(columns)]
    for c in range(columns):
        at = slice(c * CELL, (c + 1) * CELL)
        for p in range(rows // SUB):
            top = slice(p * SUB, (p + 1) * SUB)
            values, weight_iv, base = [], [], []
            for e, (_, _, epoch, _) in enumerate(units):
                value = late[c][e]
                values.append(value.astype(jnp.float32)[top])
                iv = inv_var[epoch, :, at].astype(jnp.float32)[top]
                weight_iv.append(iv)
                base.append(clip_mask[epoch, top, at].astype(jnp.float32) * iv)
            num = tree_sum(b * v for b, v in zip(base, values))
            den = tree_sum(base)
            mean = num / (1.0 + den)
            for sweep in range(ITERS):
                weight = []
                for e in range(epochs):
                    resid = values[e] - mean
                    weight.append(base[e] / (1.0 + weight_iv[e] * resid * resid))
                num = tree_sum(w * v for w, v in zip(weight, values))
                den = tree_sum(weight)
                mean = num / (1.0 + den)
            out[top, at] = num / jnp.sqrt(1.0 + den)


def stack(count, steps, blocks, basis, clip_mask, inv_var):
    epochs, rows, width = clip_mask.shape
    return pl.pallas_call(
        functools.partial(stack_kernel, count, steps),
        out_shape=jax.ShapeDtypeStruct((rows, width), jnp.float32),
        compiler_params=pltpu.CompilerParams(vmem_limit_bytes=VMEM_LIMIT),
        cost_estimate=pl.CostEstimate(
            flops=100 * epochs * rows * width, bytes_accessed=10**6, transcendentals=0
        ),
    )(*blocks, basis, clip_mask, inv_var)


def exchange(block, step):
    count = lax.axis_size("epoch")
    apart = (step, step) if isinstance(step, int) else step
    return lax.ppermute(block, "epoch", [(i, i ^ (2 * apart[i % 2])) for i in range(count)])


def swap_cores(block):
    return lax.ppermute(block, "epoch", [(i, i ^ 1) for i in range(lax.axis_size("epoch"))])


def local(science, template, kernels, coef, grid_index, clip_mask, inv_var):
    rows, width = template.shape
    chips = lax.axis_size("epoch") // 2
    view = (chips, 2, rows, width)
    pairs = [(k, k - 1) for k in range(chips - 1, 1, -2)]
    pairs.sort(key=lambda step: not with_template(step[0]))
    steps = [0] + pairs + [1]
    pair_science = swap_cores(science).reshape(view)
    pair_coef = swap_cores(coef)[0]
    pair_index = swap_cores(grid_index)[0]
    pair = swap_cores(template)
    own, edge, table = stage(science.reshape(view), template, coef[0], grid_index[0], nothing())
    sent = pack(steps, own, pair_science, table, pair_coef, pair_index, edge, pair)
    arrived = [exchange(block, step) for step, block in zip(steps[1:], sent[1:])]
    near, near_steps, swapped = [], [], {}
    for step, block in zip(steps[1:], arrived):
        if isinstance(step, int):
            first = block_rows(step, rows, width // CELL)[0]
            near.append(edge_rows(block, first, rows, width))
            near_steps.append(step)
        elif with_template(step[0]):
            swapped[step] = swap_cores(block)
            near += [block, swapped[step]]
            near_steps.append(step)
    basis = basis_rows(kernels, template, pair, near, near_steps)
    blocks = [sent[0]]
    for step, block in zip(steps[1:], arrived):
        blocks.append(block)
        if not isinstance(step, int):
            if step not in swapped:
                swapped[step] = swap_cores(pass_on(block, near[-1]))
            blocks.append(swapped[step])
    return stack(kernels.shape[0], steps, blocks, basis, clip_mask, inv_var)


def solution(mesh):
    return jax.shard_map(
        local,
        mesh=mesh,
        in_specs=(
            P(("groups", "epoch"), None, None),
            P(("groups", "epoch"), None),
            P(),
            P(("groups", "epoch"), None, None),
            P(("groups", "epoch"), None, None),
            P("groups", "epoch", None),
            P("groups", "epoch", None),
        ),
        out_specs=P(("groups", "epoch"), None),
        check_vma=False,
    )
```

```python
import functools

import jax
import jax.numpy as jnp
from jax import lax
from jax.experimental import pallas as pl
from jax.experimental.pallas import tpu as pltpu
from jax.sharding import PartitionSpec as P

CELL = 128
ITERS = 3
LANES = 128
SUB = 8
TILE = 16
VMEM_LIMIT = 16 * 1024 * 1024


def up(value, unit):
    return -(-value // unit) * unit


def tree_sum(items):
    items = list(items)
    while len(items) > 1:
        items = [
            items[i] + items[i + 1] if i + 1 < len(items) else items[i]
            for i in range(0, len(items), 2)
        ]
    return items[0]


def cell_rows(coef, grid_index):
    levels, basis = coef.shape
    level = lax.broadcasted_iota(jnp.int32, (levels, basis), 0)
    picked = []
    for r in range(grid_index.shape[0]):
        for c in range(grid_index.shape[1]):
            chosen = jnp.broadcast_to(grid_index[r : r + 1, c : c + 1], (levels, basis)) == level
            picked.append(jnp.sum(jnp.where(chosen, coef[...], 0.0), axis=0, keepdims=True))
    table = jnp.concatenate(picked, axis=0)
    table = jnp.concatenate(
        [table, jnp.zeros((table.shape[0], LANES - basis), jnp.float32)], axis=1
    )
    first = table.astype(jnp.bfloat16).astype(jnp.float32)
    rest = table - first
    second = rest.astype(jnp.bfloat16).astype(jnp.float32)
    third = rest - second
    return first + pltpu.roll(second, basis, 1) + pltpu.roll(third, 2 * basis, 1)


def with_template(k):
    return k & (k + 1) == 0 and k > 0


def handled(step, core):
    return step if isinstance(step, int) else jnp.where(core == 0, step[0], step[1])


def block_rows(step, rows, columns):
    cores = 1 if isinstance(step, int) else 2
    first = cores * 2 * columns * rows
    size = up(2 * columns, SUB)
    tail = first + (columns * rows if with_template(step if cores == 1 else step[1]) else 0)
    return first, tail, tail + size


def stage_kernel(science, template, coef, grid_index, first, out, edge, table):
    out[...] = science[...]
    edge[...] = template[...]
    table[...] = cell_rows(coef, grid_index)


def nothing_kernel(out):
    out[...] = jnp.zeros(out.shape, jnp.float32)


def nothing():
    return pl.pallas_call(
        nothing_kernel,
        out_shape=jax.ShapeDtypeStruct((SUB, LANES), jnp.float32),
        compiler_params=pltpu.CompilerParams(vmem_limit_bytes=VMEM_LIMIT),
        cost_estimate=pl.CostEstimate(flops=1000000000, bytes_accessed=4096, transcendentals=0),
    )()


def stage(science, template, coef, grid_index, first):
    chips, _, rows, width = science.shape
    return pl.pallas_call(
        stage_kernel,
        out_shape=[
            jax.ShapeDtypeStruct(science.shape, jnp.bfloat16),
            jax.ShapeDtypeStruct(template.shape, jnp.bfloat16),
            jax.ShapeDtypeStruct((grid_index.shape[0] * grid_index.shape[1], LANES), jnp.float32),
        ],
        compiler_params=pltpu.CompilerParams(vmem_limit_bytes=VMEM_LIMIT),
        cost_estimate=pl.CostEstimate(flops=0, bytes_accessed=1_000_000, transcendentals=0),
    )(science, template, coef, grid_index, first)


def pack_kernel(
    steps, own, pair, own_table, pair_coef, pair_index, own_template, pair_template, *refs
):
    blocks, tables = refs[:-1], refs[-1]
    rows, width = own_template.shape
    columns = width // CELL
    me = lax.axis_index("epoch")
    core, here = lax.rem(me, 2), lax.div(me, 2)
    half = tables.shape[0] // 2
    cells = own_table.shape[0]
    tables[:cells] = own_table[...]
    tables[half : half + cells] = cell_rows(pair_coef, pair_index)
    for step, block in zip(steps, blocks):
        to = here ^ handled(step, core)
        edge, tail, _ = block_rows(step, rows, columns)
        first = 0
        for target in [core] if isinstance(step, int) else range(2):
            for source in (own, pair):
                for c in range(columns):
                    block[first : first + rows] = source[
                        to, target, :, c * CELL : (c + 1) * CELL
                    ]
                    first += rows
        if edge < tail:
            mine, other = own_template[...], pair_template[...]
            near = other.astype(jnp.float32)
            if not isinstance(step, int):
                near = jnp.where(here < to, mine.astype(jnp.float32), near)
            for c in range(columns):
                at = slice(c * CELL, (c + 1) * CELL)
                block[edge + c * rows : edge + (c + 1) * rows] = near[:, at].astype(jnp.bfloat16)
        cell_row = lax.div(to * 2 * rows, CELL)
        picked = [
            tables[pl.ds(q * half + cell_row * columns + c, 1), :]
            for q in range(2)
            for c in range(columns)
        ]
        spare = up(2 * columns, SUB) - 2 * columns
        if spare:
            picked.append(jnp.zeros((spare, LANES), jnp.float32))
        block[tail:] = jnp.concatenate(picked, axis=0).astype(jnp.bfloat16)


def pack(steps, own, pair, own_table, pair_coef, pair_index, own_template, pair_template):
    rows, width = own_template.shape
    columns = width // CELL
    assert CELL % (2 * rows) == 0
    half = up(own_table.shape[0], SUB)
    return pl.pallas_call(
        functools.partial(pack_kernel, steps),
        out_shape=[
            jax.ShapeDtypeStruct((block_rows(step, rows, columns)[2], LANES), jnp.bfloat16)
            for step in steps
        ],
        scratch_shapes=[pltpu.VMEM((2 * half, LANES), jnp.float32)],
        compiler_params=pltpu.CompilerParams(vmem_limit_bytes=VMEM_LIMIT),
        cost_estimate=pl.CostEstimate(flops=0, bytes_accessed=500_000, transcendentals=0),
    )(own, pair, own_table, pair_coef, pair_index, own_template, pair_template)


def edge_kernel(first, block, out):
    rows, width = out.shape
    for c in range(width // CELL):
        out[:, c * CELL : (c + 1) * CELL] = block[first + c * rows : first + (c + 1) * rows]


def edge_rows(block, first, rows, width):
    return pl.pallas_call(
        functools.partial(edge_kernel, first),
        out_shape=jax.ShapeDtypeStruct((rows, width), jnp.bfloat16),
        compiler_params=pltpu.CompilerParams(vmem_limit_bytes=VMEM_LIMIT),
        cost_estimate=pl.CostEstimate(flops=10_000_000, bytes_accessed=60_000, transcendentals=0),
    )(block)


def pass_kernel(block, after, out):
    out[...] = block[...]


def pass_on(block, after):
    return pl.pallas_call(
        pass_kernel,
        out_shape=jax.ShapeDtypeStruct(block.shape, block.dtype),
        compiler_params=pltpu.CompilerParams(vmem_limit_bytes=VMEM_LIMIT),
        cost_estimate=pl.CostEstimate(flops=0, bytes_accessed=100_000, transcendentals=0),
    )(block, after)


def basis_kernel(slot, steps, kernels, own, pair, *refs):
    held, (out, image, left, right) = refs[:-4], refs[-4:]
    side, count, _ = kernels.shape
    half = side // 2
    rows, width = own.shape
    columns = width // CELL
    span = image.shape[1]
    me = lax.axis_index("epoch")
    odd, here = lax.rem(me, 2) == 1, lax.div(me, 2)
    want = jnp.where(odd, here + 1, here - 1)
    image[...] = jnp.zeros(image.shape, jnp.float32)
    near = pair[...].astype(jnp.float32)
    far = jnp.zeros(own.shape, jnp.float32)
    held = list(held)
    for step in steps:
        at = block_rows(step, rows, columns)[0]
        found = []
        for _ in range(1 if isinstance(step, int) else 2):
            block = held.pop(0)
            if isinstance(step, int):
                found.append(block[...].astype(jnp.float32))
                continue
            lines = [block[at + c * rows : at + (c + 1) * rows] for c in range(columns)]
            found.append(jnp.concatenate([line.astype(jnp.float32) for line in lines], axis=1))
        line = found[0] if len(found) == 1 else jnp.where(odd, found[0], found[1])
        k = step if isinstance(step, int) else step[1]
        far = jnp.where(here ^ k == want, line, far)
    low = jnp.where(odd, near, far)
    high = jnp.where(odd, far, near)
    image[:half, :width] = low[rows - half :, :]
    image[half : half + rows, :width] = own[...].astype(jnp.float32)
    image[half + rows : 2 * half + rows, :width] = high[:half, :]
    image[...] = pltpu.roll(image[...], (span + half + 1 - slot) % span, 1)
    flip = (
        lax.broadcasted_iota(jnp.int32, (side, LANES), 0)
        + lax.broadcasted_iota(jnp.int32, (side, LANES), 1)
        == slot - 1
    ).astype(jnp.float32).astype(jnp.bfloat16)
    per = LANES // slot
    lines = [
        jnp.dot(kernels[u], flip, preferred_element_type=jnp.float32) for u in range(side)
    ]
    left[...] = jnp.zeros(left.shape, jnp.bfloat16)
    for phase in range(min(per, rows)):
        chunks = {}
        for u in range(side):
            chunk, place = divmod(u + phase, per)
            line = lines[u] if place == 0 else pltpu.roll(lines[u], place * slot, 1)
            chunks[chunk] = line if chunk not in chunks else chunks[chunk] + line
        for y in range(phase, rows, per):
            for chunk, value in chunks.items():
                at = (y // per + chunk) * LANES
                left[y * count : (y + 1) * count, at : at + LANES] = value.astype(jnp.bfloat16)
    for row in range(rows + 2 * half):
        line = jnp.broadcast_to(image[row : row + 1, :], (slot, span))
        moved = pltpu.roll(line, 0, 1, stride=1, stride_axis=0)
        right[row * slot : (row + 1) * slot, :] = moved[:, :width].astype(jnp.bfloat16)
    out[...] = jnp.dot(
        left[...], right[...], preferred_element_type=jnp.float32
    ).astype(jnp.bfloat16)


def basis_rows(kernels, own, pair, held, steps):
    count, side, _ = kernels.shape
    rows, width = own.shape
    slot = up(side, 32)
    lines = rows + side - 1
    span = up(width + side, LANES)
    depth = up(lines * slot, LANES)
    return pl.pallas_call(
        functools.partial(basis_kernel, slot, steps),
        out_shape=jax.ShapeDtypeStruct((rows * count, width), jnp.bfloat16),
        scratch_shapes=[
            pltpu.VMEM((up(lines, SUB), span), jnp.float32),
            pltpu.VMEM((rows * count, depth), jnp.bfloat16),
            pltpu.VMEM((depth, width), jnp.bfloat16),
        ],
        compiler_params=pltpu.CompilerParams(vmem_limit_bytes=VMEM_LIMIT),
        cost_estimate=pl.CostEstimate(
            flops=2 * rows * count * depth * width, bytes_accessed=600_000, transcendentals=0
        ),
    )(kernels.transpose(1, 0, 2), own, pair, *held)


def unit_terms(count, steps, blocks, rows, columns):
    me = lax.axis_index("epoch")
    core, here = lax.rem(me, 2), lax.div(me, 2)
    size = up(2 * columns, SUB)
    tails = jnp.concatenate([block[block.shape[0] - size :] for block in blocks], axis=0)
    shape = (LANES, 3 * LANES)
    target = lax.broadcasted_iota(jnp.int32, shape, 1)
    target = lax.div(target, LANES) * count + lax.rem(target, count)
    spread = lax.broadcasted_iota(jnp.int32, shape, 0) == target
    tiled = jnp.dot(
        tails,
        spread.astype(jnp.float32).astype(jnp.bfloat16),
        preferred_element_type=jnp.float32,
    )
    found = []
    for step in steps:
        for carrier in [core] if isinstance(step, int) else [core, 1 - core]:
            i = len(found) // 2
            chip = here ^ handled(step, carrier)
            base = 0 if isinstance(step, int) else core * (2 * columns * rows)
            for j in range(2):
                first = i * size + j * columns
                terms = [
                    tiled[first : first + columns, term * LANES : (term + 1) * LANES]
                    for term in range(3)
                ]
                start = base + j * columns * rows
                found.append((blocks[i], start, chip * 2 + (carrier ^ j), terms))
    return found


def cell_differences(count, units, basis, rows, columns, c):
    at = slice(c * CELL, (c + 1) * CELL)
    parts = rows // SUB
    depth = SUB * count
    lane = lax.broadcasted_iota(jnp.int32, (SUB, LANES), 1)
    line = lax.broadcasted_iota(jnp.int32, (SUB, LANES), 0)
    diagonal = (lane >= line * count) & (lane < (line + 1) * count)
    weights = [
        jnp.concatenate(
            [
                jnp.where(diagonal, jnp.broadcast_to(unit[3][term][c : c + 1], (SUB, LANES)), 0.0)
                for unit in units
            ],
            axis=0,
        ).astype(jnp.bfloat16)
        for term in range(3)
    ]
    planes = jnp.concatenate([basis[p * depth : (p + 1) * depth, at] for p in range(parts)], axis=1)
    model = jnp.dot(
        jnp.concatenate(weights, axis=1),
        jnp.concatenate([planes] * 3, axis=0),
        preferred_element_type=jnp.float32,
    )
    values = []
    for e, (block, start, _, _) in enumerate(units):
        first = start + c * rows
        first = first if isinstance(first, int) else pl.multiple_of(first, rows)
        science = block[pl.ds(first, rows), :].astype(jnp.float32)
        planes = [model[e * SUB : (e + 1) * SUB, p * CELL : (p + 1) * CELL] for p in range(parts)]
        values.append((science - jnp.concatenate(planes, axis=0)).astype(jnp.bfloat16))
    return values


def stack_kernel(count, steps, *refs):
    blocks = refs[:-4]
    basis, clip_mask, inv_var, out = refs[-4:]
    epochs, rows, width = clip_mask.shape
    columns = width // CELL
    units = unit_terms(count, steps, blocks, rows, columns)
    late = [cell_differences(count, units, basis, rows, columns, c) for c in range(columns)]
    for c in range(columns):
        at = slice(c * CELL, (c + 1) * CELL)
        for p in range(rows // SUB):
            top = slice(p * SUB, (p + 1) * SUB)
            values, weight_iv, base = [], [], []
            for e, (_, _, epoch, _) in enumerate(units):
                value = late[c][e]
                values.append(value.astype(jnp.float32)[top])
                iv = inv_var[epoch, :, at].astype(jnp.float32)[top]
                weight_iv.append(iv)
                base.append(clip_mask[epoch, top, at].astype(jnp.float32) * iv)
            num = tree_sum(b * v for b, v in zip(base, values))
            den = tree_sum(base)
            mean = num / (1.0 + den)
            for sweep in range(ITERS):
                weight = []
                for e in range(epochs):
                    resid = values[e] - mean
                    weight.append(base[e] / (1.0 + weight_iv[e] * resid * resid))
                num = tree_sum(w * v for w, v in zip(weight, values))
                den = tree_sum(weight)
                mean = num / (1.0 + den)
            out[top, at] = num / jnp.sqrt(1.0 + den)


def stack(count, steps, blocks, basis, clip_mask, inv_var):
    epochs, rows, width = clip_mask.shape
    return pl.pallas_call(
        functools.partial(stack_kernel, count, steps),
        out_shape=jax.ShapeDtypeStruct((rows, width), jnp.float32),
        compiler_params=pltpu.CompilerParams(vmem_limit_bytes=VMEM_LIMIT),
        cost_estimate=pl.CostEstimate(
            flops=100 * epochs * rows * width, bytes_accessed=10**6, transcendentals=0
        ),
    )(*blocks, basis, clip_mask, inv_var)


def exchange(block, step):
    count = lax.axis_size("epoch")
    apart = (step, step) if isinstance(step, int) else step
    return lax.ppermute(block, "epoch", [(i, i ^ (2 * apart[i % 2])) for i in range(count)])


def swap_cores(block):
    return lax.ppermute(block, "epoch", [(i, i ^ 1) for i in range(lax.axis_size("epoch"))])


def local(science, template, kernels, coef, grid_index, clip_mask, inv_var):
    rows, width = template.shape
    chips = lax.axis_size("epoch") // 2
    view = (chips, 2, rows, width)
    pairs = [(k - 1, k) for k in range(chips - 1, 1, -2)]
    pairs.sort(key=lambda step: not with_template(step[1]))
    steps = [0] + pairs + [1]
    pair_science = swap_cores(science).reshape(view)
    pair_coef = swap_cores(coef)[0]
    pair_index = swap_cores(grid_index)[0]
    pair = swap_cores(template)
    own, edge, table = stage(science.reshape(view), template, coef[0], grid_index[0], nothing())
    sent = pack(steps, own, pair_science, table, pair_coef, pair_index, edge, pair)
    arrived = [exchange(block, step) for step, block in zip(steps[1:], sent[1:])]
    near, near_steps, swapped = [], [], {}
    for step, block in zip(steps[1:], arrived):
        if isinstance(step, int):
            first = block_rows(step, rows, width // CELL)[0]
            near.append(edge_rows(block, first, rows, width))
            near_steps.append(step)
        elif with_template(step[1]):
            swapped[step] = swap_cores(block)
            near += [block, swapped[step]]
            near_steps.append(step)
    basis = basis_rows(kernels, template, pair, near, near_steps)
    blocks = [sent[0]]
    for step, block in zip(steps[1:], arrived):
        blocks.append(block)
        if not isinstance(step, int):
            if step not in swapped:
                swapped[step] = swap_cores(pass_on(block, near[-1]))
            blocks.append(swapped[step])
    return stack(kernels.shape[0], steps, blocks, basis, clip_mask, inv_var)


def solution(mesh):
    return jax.shard_map(
        local,
        mesh=mesh,
        in_specs=(
            P(("groups", "epoch"), None, None),
            P(("groups", "epoch"), None),
            P(),
            P(("groups", "epoch"), None, None),
            P(("groups", "epoch"), None, None),
            P("groups", "epoch", None),
            P("groups", "epoch", None),
        ),
        out_specs=P(("groups", "epoch"), None),
        check_vma=False,
    )
```
